32 devices in a mesh: parts: 2 (over y), rung: 2 (over x), ty: 4 (over z), tx: 2 (over core).
Axes of the slice: x: 2, y: 2, z: 4, core: 2. Of those that a mesh axis runs over, the one named last changes fastest.
Arguments:
- potential: float32 [64, 32, 256], P('parts', 'ty', 'tx'), parts along dimension 0, may hold values from 0 to 3
- labels: int32 [64, 32, 256], P('parts', 'ty', 'tx'), parts along dimension 0, may hold values 0 or 1
- rung_mu: int32 [4], P(('parts', 'rung')), parts along dimension 0, may hold values from 0 to 7
- mu_table: float32 [8], replicated, may hold values from -8.5 to -6.5
- target_table: float32 [8], replicated, may hold values from 0.5 to 1
Outputs:
- potential_grad: float32 [64, 32, 256], P('parts', 'ty', 'tx'), parts along dimension 0
The draws below stay inside these ranges and needn't reach their ends.
There are 2 independent parts, one for each index of `parts`. The reference program is written for one: setup_inputs(seed, part) draws one part's arguments, and reference() takes and returns one part's arrays. A program takes and returns all parts, laid end to end along the dimension named above; an argument that names none is the same for every part. Nothing has to cross between parts.
All inputs are finite; a program needn't handle non-finite values. No bound on the sum of `labels` on one device may be relied on, other than what follows from the above.
Results may differ from the reference program's by a relative error of at most 0.0003.
Values sent between devices are 32-bit elements; how exact they have to be, the bound alone decides.
A program may use at most 64 MiB of HBM per device.

```python
import math
import jax
import jax.numpy as jnp
from jax import lax

PL = 32
RADIUS = 4
NMU = 8
NRUNG = 2
NY = 32
NX = 256
CELLS = 262144


def draw_potential(key, part):
    key_rough = jax.random.fold_in(key, 0)
    row_index = jnp.arange(NY, dtype=jnp.float32)
    incline = 1.1 * (1.0 - row_index / (NY - 1))
    rough_part = jax.random.uniform(key_rough, (PL, NY, NX), jnp.float32)
    return incline[None, :, None] + 1.5 * rough_part


def plant(result, rng, smallest, high):
    spot = [jax.random.randint(jax.random.fold_in(rng, axis), (), 0, length) for axis, length in enumerate(result.shape)]
    main_axis = result.shape.index(max(result.shape))
    neighbour = spot[:main_axis] + [(spot[main_axis] + 1) % result.shape[main_axis]] + spot[main_axis + 1:]
    return result.at[tuple(spot)].set(smallest).at[tuple(neighbour)].set(high)


def setup_inputs(seed: int = 0, part: int = 0) -> dict:
    arg_keys = jax.random.split(jax.random.key(seed), 6)
    own_keys = jax.random.split(jax.random.fold_in(arg_keys[5], part), 6)
    potential = draw_potential(jax.random.fold_in(jax.random.fold_in(arg_keys[5], part), 71), part)
    labels = plant((jax.random.randint(own_keys[1], (PL, NY, NX), 0, 4) < 3).astype(jnp.int32), jax.random.fold_in(own_keys[1], 1), 0, 1)
    rung_mu = jax.random.randint(own_keys[2], (NRUNG,), 0, NMU).astype(jnp.int32)
    mu_table = jnp.clip(jax.random.uniform(arg_keys[3], (NMU,), jnp.float32, -8.5, -6.5), -8.5, -6.5)
    target_table = jnp.clip(jax.random.uniform(arg_keys[4], (NMU,), jnp.float32, 0.5, 1.0), 0.5, 1.0)
    return {"potential": potential, "labels": labels, "rung_mu": rung_mu, "mu_table": mu_table, "target_table": target_table}


def reach_of(allowed, factor, radius):
    height = -1
    for candidate in range(radius + 1):
        if factor * candidate * candidate <= allowed:
            height = candidate
    return height

def span_count(height):
    return 2 * height + 1 if height >= 0 else 0

def stencil_tables(radius):
    entries = []
    shell_count = 0
    for plane_off in range(-radius, radius + 1):
        for row_off in range(-radius, radius + 1):
            square = plane_off * plane_off + row_off * row_off
            ball_reach = reach_of(radius * radius - square, 1, radius)
            inner_reach = reach_of((2 * radius - 1) ** 2 - 4 * square, 4, radius)
            outer_reach = reach_of((2 * radius + 1) ** 2 - 4 * square, 4, radius)
            shell_count += span_count(outer_reach) - span_count(inner_reach)
            if ball_reach >= 0 or outer_reach > inner_reach:
                entries.append((plane_off, row_off, ball_reach, inner_reach, outer_reach))
    return (entries, shell_count)

def box_sums(source, moments):
    span_width = source.shape[-1] - 2 * RADIUS
    center = source[..., RADIUS:RADIUS + span_width]
    box_list = [center]
    moment_list = [jnp.zeros_like(center)]
    for height in range(1, RADIUS + 1):
        right_part = source[..., RADIUS + height:RADIUS + height + span_width]
        left_part = source[..., RADIUS - height:RADIUS - height + span_width]
        box_list.append(box_list[-1] + right_part + left_part)
        if moments:
            moment_list.append(moment_list[-1] + height * (right_part - left_part))
    return (box_list, moment_list)

def window(source, plane_off, row_off):
    planes = source.shape[-3] - 2 * RADIUS
    row_count = source.shape[-2] - 2 * RADIUS
    plane_start = RADIUS + plane_off
    row_start = RADIUS + row_off
    return source[..., plane_start:plane_start + planes, row_start:row_start + row_count, :]

def shell_of(source_list, inner_reach, outer_reach):
    if inner_reach >= 0:
        return source_list[outer_reach] - source_list[inner_reach]
    return source_list[outer_reach]

def spread(grid_field):
    entries, shell_count = stencil_tables(RADIUS)
    area_scale = 4.0 * math.pi * RADIUS * RADIUS / shell_count
    box_list, moment_list = box_sums(grid_field, True)
    volume = jnp.zeros_like(window(box_list[0], 0, 0))
    surface = jnp.zeros_like(volume)
    along_plane = jnp.zeros_like(volume)
    along_row = jnp.zeros_like(volume)
    along_col = jnp.zeros_like(volume)
    for stencil_row in entries:
        plane_off, row_off, ball_reach, inner_reach, outer_reach = stencil_row
        if ball_reach >= 0:
            volume = volume + window(box_list[ball_reach], plane_off, row_off)
        if outer_reach > inner_reach:
            shell_part = window(shell_of(box_list, inner_reach, outer_reach), plane_off, row_off)
            surface = surface + shell_part
            along_plane = along_plane + plane_off * shell_part
            along_row = along_row + row_off * shell_part
            along_col = along_col + window(shell_of(moment_list, inner_reach, outer_reach), plane_off, row_off)
    vector_scale = area_scale / RADIUS
    return (volume, area_scale * surface, vector_scale * along_plane, vector_scale * along_row, vector_scale * along_col)

def collect(fields):
    entries, shell_count = stencil_tables(RADIUS)
    area_scale = 4.0 * math.pi * RADIUS * RADIUS / shell_count
    box_list, unused_list = box_sums(fields[0:4], False)
    unused_boxes, moment_list = box_sums(fields[4], True)
    total = jnp.zeros_like(window(box_list[0][0], 0, 0))
    vector_scale = area_scale / RADIUS
    for stencil_row in entries:
        plane_off, row_off, ball_reach, inner_reach, outer_reach = stencil_row
        if ball_reach >= 0:
            total = total + window(box_list[ball_reach][0], plane_off, row_off)
        if outer_reach > inner_reach:
            shell_part = window(shell_of(box_list, inner_reach, outer_reach), plane_off, row_off)
            shell_moment = window(shell_of(moment_list, inner_reach, outer_reach), plane_off, row_off)
            total = total + area_scale * shell_part[1] - vector_scale * (plane_off * shell_part[2] + row_off * shell_part[3] + shell_moment)
    return total

def energy(volume, surface, vec_plane, vec_row, vec_col):
    free_volume = 1.0 - volume
    vector_sq = vec_plane * vec_plane + vec_row * vec_row + vec_col * vec_col
    first_term = -surface / (4.0 * math.pi * RADIUS * RADIUS) * jnp.log(free_volume)
    second_term = (surface * surface - vector_sq) / (4.0 * math.pi * RADIUS * free_volume)
    third_term = (surface * surface * surface - 3.0 * surface * vector_sq) / (24.0 * math.pi * free_volume * free_volume)
    return first_term + second_term + third_term

def total_energy(densities):
    return jnp.sum(energy(*densities))

def derivatives(densities):
    return jax.grad(total_energy)(densities)

def hess_apply(densities, vector):
    return jax.vjp(derivatives, densities)[1](vector)[0]

def lookup(table_vals, chosen):
    return jnp.sum(jnp.where(jnp.arange(table_vals.shape[0]) == chosen, table_vals, 0.0))

def pad_planes(grid_field):
    leading = [(0, 0)] * (grid_field.ndim - 3)
    return jnp.pad(grid_field, leading + [(RADIUS, RADIUS), (0, 0), (0, 0)])

def pad_wrap(grid_field):
    leading = [(0, 0)] * (grid_field.ndim - 3)
    wrapped = jnp.pad(grid_field, leading + [(0, 0), (RADIUS, RADIUS), (RADIUS, RADIUS)], mode='wrap')
    return pad_planes(wrapped)

def reference(potential, labels, rung_mu, mu_table, target_table):
    pore_mask = labels.astype(jnp.float32)

    def one_rung(rung_index):
        chem_pot = lookup(mu_table, rung_index)
        target = lookup(target_table, rung_index)
        rho_start = pore_mask * jnp.exp(chem_pot - potential)
        densities = spread(pad_wrap(rho_start))
        derivs = derivatives(densities)
        correlation = -collect(pad_wrap(jnp.stack(derivs)))
        weight = pore_mask * jnp.exp(correlation - potential)
        amount = jnp.sum(weight) / CELLS
        coefficient = jnp.log(amount / target) / amount
        images = spread(pad_wrap(weight))
        adjoints = hess_apply(densities, images)
        pulled_back = collect(pad_wrap(jnp.stack(adjoints)))
        return coefficient * (rho_start * pulled_back - weight)
    rung_grads = lax.map(one_rung, rung_mu)
    return lax.optimization_barrier(jnp.sum(rung_grads, axis=0))
```

```python
import functools
import math

import numpy as np
import ml_dtypes

import jax
import jax.numpy as jnp
from jax import lax
from jax.experimental import pallas as pl
from jax.experimental.pallas import tpu as pltpu
from jax.sharding import PartitionSpec as P

RADIUS = 4
ROWS = 8
TALL = 24
MID = 16
LANES = 128
WIDE = 256
KINDS = 2 * RADIUS + 1
DEPTH = 224
COEF_A = 1.0 / (4.0 * math.pi * RADIUS * RADIUS)
COEF_B = 1.0 / (4.0 * math.pi * RADIUS)
COEF_C = 1.0 / (24.0 * math.pi)


def reach_of(allowed, factor, radius):
    height = -1
    for candidate in range(radius + 1):
        if factor * candidate * candidate <= allowed:
            height = candidate
    return height


def span_count(height):
    return 2 * height + 1 if height >= 0 else 0


def reaches(plane_off, row_off):
    square = plane_off * plane_off + row_off * row_off
    ball = reach_of(RADIUS * RADIUS - square, 1, RADIUS)
    inner = reach_of((2 * RADIUS - 1) ** 2 - 4 * square, 4, RADIUS)
    outer = reach_of((2 * RADIUS + 1) ** 2 - 4 * square, 4, RADIUS)
    return ball, inner, outer


OFFS = range(-RADIUS, RADIUS + 1)
SHELL = sum(
    span_count(reaches(p, s)[2]) - span_count(reaches(p, s)[1]) for p in OFFS for s in OFFS
)
AREA = 4.0 * math.pi * RADIUS * RADIUS / SHELL
VEC = AREA / RADIUS


def shell_terms(p, s):
    _, inner, outer = reaches(p, s)
    terms = []
    if outer >= 0:
        terms.append((outer, 1))
    if inner >= 0:
        terms.append((inner, -1))
    return terms


def column_matrix():
    mat = np.zeros((KINDS, WIDE, WIDE), np.float32)
    for out in range(WIDE):
        for h in OFFS:
            src = (out + h) % WIDE
            for k in range(abs(h), RADIUS + 1):
                mat[k, src, out] = 1
                if k > 0:
                    mat[RADIUS + k, src, out] = h
    return mat


def spread_rows():
    mat = np.zeros((4, RADIUS + 1, MID, DEPTH), np.float32)
    for p in range(RADIUS + 1):
        for s in OFFS:
            ball = reaches(p, s)[0]
            for r in range(MID):
                src = r + RADIUS + s
                if ball >= 0:
                    mat[0, p, r, ball * TALL + src] += 1
                for k, sign in shell_terms(p, s):
                    mat[1, p, r, k * TALL + src] += sign
                    mat[2, p, r, k * TALL + src] += s * sign
                    if k > 0:
                        mat[3, p, r, (RADIUS + k) * TALL + src] += sign
    flat = mat.reshape(4 * (RADIUS + 1) * MID, DEPTH)
    return np.concatenate([flat, flat], axis=1)


def collect_rows():
    full = np.zeros((KINDS, KINDS, ROWS, 5 * MID), np.float32)
    for p in OFFS:
        for s in OFFS:
            ball = reaches(p, s)[0]
            for r in range(ROWS):
                src = r + RADIUS + s
                if ball >= 0:
                    full[ball, p + RADIUS, r, src] += 1
                for k, sign in shell_terms(p, s):
                    full[k, p + RADIUS, r, MID + src] += sign
                    full[k, p + RADIUS, r, 2 * MID + src] += p * sign
                    full[k, p + RADIUS, r, 3 * MID + src] += s * sign
                    if k > 0:
                        full[RADIUS + k, p + RADIUS, r, 4 * MID + src] += sign
    used = [(k, p) for k in range(KINDS) for p in range(KINDS) if np.any(full[k, p])]
    flat = np.concatenate([full[k, p] for k, p in used], axis=0)
    return used, np.concatenate([flat, flat], axis=1)


COLS = column_matrix()
USED, BACK = collect_rows()
GROUPS = 4 * (RADIUS + 1)
BF = ml_dtypes.bfloat16
COLS_FWD = np.concatenate([COLS[k] for k in range(1, KINDS)], axis=1).astype(BF)
COLS_BACK = np.concatenate([COLS[k][:, :LANES] for k in range(KINDS)], axis=0).astype(BF)
FRONT = spread_rows().astype(BF)
BACK = BACK.astype(BF)
N_BACK = len(USED) * ROWS


def split(x):
    high = x.astype(jnp.bfloat16)
    low = (x - high.astype(jnp.float32)).astype(jnp.bfloat16)
    return high, low


def dot(a, b):
    return jnp.dot(a, b, preferred_element_type=jnp.float32)


def columns_forward(planes, x_ref, cols_ref, c_ref):
    x = x_ref[...].reshape(planes * TALL, WIDE)
    c_ref[:, 0:WIDE] = x
    high, low = split(x)
    for k in range(1, KINDS):
        mat = cols_ref[:, (k - 1) * WIDE : k * WIDE]
        c_ref[:, k * WIDE : (k + 1) * WIDE] = dot(high, mat) + dot(low, mat)


def rows_forward(planes, c_ref, front_ref, y_ref):
    zeros = jnp.zeros((RADIUS, GROUPS * MID, WIDE), jnp.float32)
    y_ref[0:RADIUS] = zeros
    y_ref[RADIUS + planes :] = zeros

    def step(q, carry):
        start = pl.multiple_of(q * TALL, TALL)
        parts = [c_ref[pl.ds(start, TALL), k * WIDE : (k + 1) * WIDE] for k in range(KINDS)]
        parts.append(jnp.zeros((DEPTH - KINDS * TALL, WIDE), jnp.float32))
        high, low = split(jnp.concatenate(parts, axis=0))
        y_ref[q + RADIUS] = dot(front_ref[...], jnp.concatenate([high, low], axis=0))
        return carry

    lax.fori_loop(0, planes, step, 0, unroll=4)


def densities_at(q, y_ref):
    def get(group, p, off):
        row = (group * (RADIUS + 1) + p) * MID
        return y_ref[q + RADIUS + off, row : row + MID, :]

    volume, surface, rows, cols = [get(g, 0, 0) for g in range(4)]
    plane = jnp.zeros_like(volume)
    for p in range(1, RADIUS + 1):
        volume = volume + (get(0, p, p) + get(0, p, -p))
        after, before = get(1, p, p), get(1, p, -p)
        surface = surface + (after + before)
        plane = plane + p * (after - before)
        rows = rows + (get(2, p, p) + get(2, p, -p))
        cols = cols + (get(3, p, p) + get(3, p, -p))
    return volume, AREA * surface, VEC * plane, VEC * rows, VEC * cols


def derivs_of(n3, n2, vp, vr, vc):
    free = 1.0 - n3
    inv = 1.0 / free
    sq = vp * vp + vr * vr + vc * vc
    u = n2 * n2 - sq
    w = n2 * (u - 2.0 * sq)
    d3 = inv * (COEF_A * n2 + inv * (COEF_B * u + inv * (2.0 * COEF_C) * w))
    d2 = -COEF_A * jnp.log(free) + inv * (2.0 * COEF_B * n2 + inv * (3.0 * COEF_C) * u)
    dv = -inv * (2.0 * COEF_B + inv * (6.0 * COEF_C) * n2)
    return d3, d2, dv * vp, dv * vr, dv * vc


def hess_of(dens, images):
    n3, n2, vp, vr, vc = dens
    m3, m2, mp, mr, mc = images
    inv = 1.0 / (1.0 - n3)
    sq = vp * vp + vr * vr + vc * vc
    u = n2 * n2 - sq
    w = n2 * (u - 2.0 * sq)
    vm = vp * mp + vr * mr + vc * mc
    h33 = inv * inv * (COEF_A * n2 + inv * (2.0 * COEF_B * u + inv * (6.0 * COEF_C) * w))
    h32 = inv * (COEF_A + inv * (2.0 * COEF_B * n2 + inv * (6.0 * COEF_C) * u))
    h3v = inv * inv * (2.0 * COEF_B + inv * (12.0 * COEF_C) * n2)
    h2v = 6.0 * COEF_C * inv * inv
    h22 = inv * (2.0 * COEF_B + inv * (6.0 * COEF_C) * n2)
    mix = h3v * m3 + h2v * m2
    return (
        h33 * m3 + h32 * m2 - h3v * vm,
        h32 * m3 + h22 * m2 - h2v * vm,
        -mix * vp - h22 * mp,
        -mix * vr - h22 * mr,
        -mix * vc - h22 * mc,
    )


def push_back(q, fields, back_ref, z_ref):
    g3, g2, gp, gr, gc = fields
    stacked = jnp.concatenate([g3, AREA * g2, -VEC * gp, -VEC * gr, -VEC * gc], axis=0)
    high, low = split(stacked)
    z_ref[q + RADIUS] = dot(back_ref[...], jnp.concatenate([high, low], axis=0))


def columns_back(planes, z_ref, cols_ref, d_ref):
    def step(q, carry):
        start = pl.multiple_of(q * ROWS, ROWS)
        for k in range(KINDS):
            total = None
            for place, (kind, off) in enumerate(USED):
                if kind == k:
                    term = z_ref[q + off, place * ROWS : (place + 1) * ROWS, :]
                    total = term if total is None else total + term
            d_ref[pl.ds(start, ROWS), k * WIDE : (k + 1) * WIDE] = total
        return carry

    lax.fori_loop(0, planes, step, 0, unroll=2)
    out = None
    for k in range(KINDS):
        high, low = split(d_ref[:, k * WIDE : (k + 1) * WIDE])
        mat = cols_ref[k * WIDE : (k + 1) * WIDE, :]
        term = dot(high, mat) + dot(low, mat)
        out = term if out is None else out + term
    return out.reshape(planes, ROWS, LANES)


def clear_edges(planes, z_ref):
    zeros = jnp.zeros((RADIUS, N_BACK, WIDE), jnp.float32)
    z_ref[0:RADIUS] = zeros
    z_ref[RADIUS + planes :] = zeros


def first_kernel(
    planes, x_ref, pot_ref, lab_ref, cols_ref, front_ref, back_ref, colsb_ref,
    weight_ref, dens_ref, c_ref, y_ref, z_ref, d_ref,
):
    columns_forward(planes, x_ref, cols_ref, c_ref)
    rows_forward(planes, c_ref, front_ref, y_ref)
    clear_edges(planes, z_ref)

    def step(q, carry):
        dens = densities_at(q, y_ref)
        for i in range(5):
            dens_ref[q, i * MID : (i + 1) * MID, :] = dens[i]
        push_back(q, derivs_of(*dens), back_ref, z_ref)
        return carry

    lax.fori_loop(0, planes, step, 0, unroll=2)
    total = columns_back(planes, z_ref, colsb_ref, d_ref)
    mask = lab_ref[...].astype(jnp.float32)
    weight_ref[...] = mask * jnp.exp(-total - pot_ref[...])


def second_kernel(
    planes, x_ref, dens_ref, rho_ref, coef_ref, cols_ref, front_ref, back_ref, colsb_ref,
    out_ref, c_ref, y_ref, z_ref, d_ref,
):
    columns_forward(planes, x_ref, cols_ref, c_ref)
    rows_forward(planes, c_ref, front_ref, y_ref)
    clear_edges(planes, z_ref)

    def step(q, carry):
        images = densities_at(q, y_ref)
        dens = [dens_ref[q, i * MID : (i + 1) * MID, :] for i in range(5)]
        push_back(q, hess_of(dens, images), back_ref, z_ref)
        return carry

    lax.fori_loop(0, planes, step, 0, unroll=2)
    total = columns_back(planes, z_ref, colsb_ref, d_ref)
    weight = x_ref[:, ROWS : 2 * ROWS, 0:LANES]
    out_ref[...] = coef_ref[0] * (rho_ref[...] * total - weight)


def scratch(planes):
    return [
        pltpu.VMEM((planes * TALL, KINDS * WIDE), jnp.float32),
        pltpu.VMEM((planes + 2 * RADIUS, GROUPS * MID, WIDE), jnp.float32),
        pltpu.VMEM((planes + 2 * RADIUS, N_BACK, WIDE), jnp.float32),
        pltpu.VMEM((planes * ROWS, KINDS * WIDE), jnp.float32),
    ]


PARAMS = pltpu.CompilerParams(vmem_limit_bytes=58 * 1024 * 1024)
VM = pl.BlockSpec(memory_space=pltpu.VMEM)
SM = pl.BlockSpec(memory_space=pltpu.SMEM)


def gather_tiles(tile):
    count = lax.axis_size("ty")
    ahead = [(i, (i + 1) % count) for i in range(count)]
    above = lax.ppermute(tile, "ty", ahead)
    below = lax.ppermute(tile, "ty", [(j, i) for i, j in ahead])
    tall = jnp.concatenate([above, tile, below], axis=1)
    other = lax.ppermute(tall, "tx", [(0, 1), (1, 0)])
    return jnp.concatenate([tall, other], axis=2)


def lookup(table_vals, chosen):
    return jnp.sum(jnp.where(jnp.arange(table_vals.shape[0]) == chosen, table_vals, 0.0))


def body(potential, labels, rung_mu, mu_table, target_table):
    planes = potential.shape[0]
    pore_mask = labels.astype(jnp.float32)
    chem_pot = lookup(mu_table, rung_mu[0])
    target = lookup(target_table, rung_mu[0])
    rho = pore_mask * jnp.exp(chem_pot - potential)
    mats = [jnp.asarray(m) for m in (COLS_FWD, FRONT, BACK, COLS_BACK)]
    weight, dens = pl.pallas_call(
        functools.partial(first_kernel, planes),
        out_shape=(
            jax.ShapeDtypeStruct(potential.shape, jnp.float32),
            jax.ShapeDtypeStruct((planes, 5 * MID, WIDE), jnp.float32),
        ),
        in_specs=[VM] * 7,
        out_specs=(VM, VM),
        scratch_shapes=scratch(planes),
        compiler_params=PARAMS,
    )(gather_tiles(rho), potential, labels, *mats)
    cell_total = weight.size * lax.axis_size("ty") * lax.axis_size("tx")
    amount = lax.psum(jnp.sum(weight), ("ty", "tx")) / cell_total
    coefficient = jnp.log(amount / target) / amount
    grad = pl.pallas_call(
        functools.partial(second_kernel, planes),
        out_shape=jax.ShapeDtypeStruct(potential.shape, jnp.float32),
        in_specs=[VM] * 3 + [SM] + [VM] * 4,
        out_specs=VM,
        scratch_shapes=scratch(planes),
        compiler_params=PARAMS,
    )(gather_tiles(weight), dens, rho, coefficient[None], *mats)
    return lax.psum(grad, "rung")


def solution(mesh):
    return jax.shard_map(
        body,
        mesh=mesh,
        in_specs=(P("parts", "ty", "tx"), P("parts", "ty", "tx"), P(("parts", "rung")), P(), P()),
        out_specs=P("parts", "ty", "tx"),
        check_vma=False,
    )
```

```python
import functools
import math

import numpy as np
import ml_dtypes

import jax
import jax.numpy as jnp
from jax import lax
from jax.experimental import pallas as pl
from jax.experimental.pallas import tpu as pltpu
from jax.sharding import PartitionSpec as P

RADIUS = 4
ROWS = 8
TALL = 24
MID = 16
LANES = 128
WIDE = 256
KINDS = 2 * RADIUS + 1
DEPTH = 224
COEF_A = 1.0 / (4.0 * math.pi * RADIUS * RADIUS)
COEF_B = 1.0 / (4.0 * math.pi * RADIUS)
COEF_C = 1.0 / (24.0 * math.pi)


def reach_of(allowed, factor, radius):
    height = -1
    for candidate in range(radius + 1):
        if factor * candidate * candidate <= allowed:
            height = candidate
    return height


def span_count(height):
    return 2 * height + 1 if height >= 0 else 0


def reaches(plane_off, row_off):
    square = plane_off * plane_off + row_off * row_off
    ball = reach_of(RADIUS * RADIUS - square, 1, RADIUS)
    inner = reach_of((2 * RADIUS - 1) ** 2 - 4 * square, 4, RADIUS)
    outer = reach_of((2 * RADIUS + 1) ** 2 - 4 * square, 4, RADIUS)
    return ball, inner, outer


OFFS = range(-RADIUS, RADIUS + 1)
SHELL = sum(
    span_count(reaches(p, s)[2]) - span_count(reaches(p, s)[1]) for p in OFFS for s in OFFS
)
AREA = 4.0 * math.pi * RADIUS * RADIUS / SHELL
VEC = AREA / RADIUS


def shell_terms(p, s):
    _, inner, outer = reaches(p, s)
    terms = []
    if outer >= 0:
        terms.append((outer, 1))
    if inner >= 0:
        terms.append((inner, -1))
    return terms


def column_matrix():
    mat = np.zeros((KINDS, WIDE, WIDE), np.float32)
    for out in range(WIDE):
        for h in OFFS:
            src = (out + h) % WIDE
            for k in range(abs(h), RADIUS + 1):
                mat[k, src, out] = 1
                if k > 0:
                    mat[RADIUS + k, src, out] = h
    return mat


def spread_rows():
    mat = np.zeros((4, RADIUS + 1, MID, DEPTH), np.float32)
    for p in range(RADIUS + 1):
        for s in OFFS:
            ball = reaches(p, s)[0]
            for r in range(MID):
                src = r + RADIUS + s
                if ball >= 0:
                    mat[0, p, r, ball * TALL + src] += 1
                for k, sign in shell_terms(p, s):
                    mat[1, p, r, k * TALL + src] += sign
                    mat[2, p, r, k * TALL + src] += s * sign
                    if k > 0:
                        mat[3, p, r, (RADIUS + k) * TALL + src] += sign
    flat = mat.reshape(4 * (RADIUS + 1) * MID, DEPTH)
    return np.concatenate([flat, flat], axis=1)


def collect_rows():
    full = np.zeros((KINDS, KINDS, ROWS, 5 * MID), np.float32)
    for p in OFFS:
        for s in OFFS:
            ball = reaches(p, s)[0]
            for r in range(ROWS):
                src = r + RADIUS + s
                if ball >= 0:
                    full[ball, p + RADIUS, r, src] += 1
                for k, sign in shell_terms(p, s):
                    full[k, p + RADIUS, r, MID + src] += sign
                    full[k, p + RADIUS, r, 2 * MID + src] += p * sign
                    full[k, p + RADIUS, r, 3 * MID + src] += s * sign
                    if k > 0:
                        full[RADIUS + k, p + RADIUS, r, 4 * MID + src] += sign
    used = [(k, p) for k in range(KINDS) for p in range(KINDS) if np.any(full[k, p])]
    flat = np.concatenate([full[k, p] for k, p in used], axis=0)
    return used, np.concatenate([flat, flat], axis=1)


COLS = column_matrix()
USED, BACK = collect_rows()
GROUPS = 4 * (RADIUS + 1)
BF = ml_dtypes.bfloat16
COLS_FWD = np.concatenate([COLS[k] for k in range(1, KINDS)], axis=1).astype(BF)
COLS_BACK = np.concatenate([COLS[k][:, :LANES] for k in range(KINDS)], axis=0).astype(BF)
FRONT = spread_rows().astype(BF)
BACK = BACK.astype(BF)
N_BACK = len(USED) * ROWS


def split(x):
    high = x.astype(jnp.bfloat16)
    low = (x - high.astype(jnp.float32)).astype(jnp.bfloat16)
    return high, low


def dot(a, b):
    return jnp.dot(a, b, preferred_element_type=jnp.float32)


def columns_forward(planes, x_ref, cols_ref, c_ref):
    x = x_ref[...].reshape(planes * TALL, WIDE)
    c_ref[:, 0:WIDE] = x
    high, low = split(x)
    for k in range(1, KINDS):
        mat = cols_ref[:, (k - 1) * WIDE : k * WIDE]
        c_ref[:, k * WIDE : (k + 1) * WIDE] = dot(high, mat) + dot(low, mat)


def rows_forward(planes, c_ref, front_ref, y_ref):
    zeros = jnp.zeros((RADIUS, GROUPS * MID, WIDE), jnp.float32)
    y_ref[0:RADIUS] = zeros
    y_ref[RADIUS + planes :] = zeros

    def step(q, carry):
        start = pl.multiple_of(q * TALL, TALL)
        parts = [c_ref[pl.ds(start, TALL), k * WIDE : (k + 1) * WIDE] for k in range(KINDS)]
        parts.append(jnp.zeros((DEPTH - KINDS * TALL, WIDE), jnp.float32))
        high, low = split(jnp.concatenate(parts, axis=0))
        y_ref[q + RADIUS] = dot(front_ref[...], jnp.concatenate([high, low], axis=0))
        return carry

    lax.fori_loop(0, planes, step, 0, unroll=4)


def densities_at(q, y_ref):
    def get(group, p, off):
        row = (group * (RADIUS + 1) + p) * MID
        return y_ref[q + RADIUS + off, row : row + MID, :]

    volume, surface, rows, cols = [get(g, 0, 0) for g in range(4)]
    plane = jnp.zeros_like(volume)
    for p in range(1, RADIUS + 1):
        volume = volume + (get(0, p, p) + get(0, p, -p))
        after, before = get(1, p, p), get(1, p, -p)
        surface = surface + (after + before)
        plane = plane + p * (after - before)
        rows = rows + (get(2, p, p) + get(2, p, -p))
        cols = cols + (get(3, p, p) + get(3, p, -p))
    return volume, AREA * surface, VEC * plane, VEC * rows, VEC * cols


def derivs_of(n3, n2, vp, vr, vc):
    free = 1.0 - n3
    inv = 1.0 / free
    sq = vp * vp + vr * vr + vc * vc
    u = n2 * n2 - sq
    w = n2 * (u - 2.0 * sq)
    d3 = inv * (COEF_A * n2 + inv * (COEF_B * u + inv * (2.0 * COEF_C) * w))
    d2 = -COEF_A * jnp.log(free) + inv * (2.0 * COEF_B * n2 + inv * (3.0 * COEF_C) * u)
    dv = -inv * (2.0 * COEF_B + inv * (6.0 * COEF_C) * n2)
    return d3, d2, dv * vp, dv * vr, dv * vc


def hess_of(dens, images):
    n3, n2, vp, vr, vc = dens
    m3, m2, mp, mr, mc = images
    inv = 1.0 / (1.0 - n3)
    sq = vp * vp + vr * vr + vc * vc
    u = n2 * n2 - sq
    w = n2 * (u - 2.0 * sq)
    vm = vp * mp + vr * mr + vc * mc
    h33 = inv * inv * (COEF_A * n2 + inv * (2.0 * COEF_B * u + inv * (6.0 * COEF_C) * w))
    h32 = inv * (COEF_A + inv * (2.0 * COEF_B * n2 + inv * (6.0 * COEF_C) * u))
    h3v = inv * inv * (2.0 * COEF_B + inv * (12.0 * COEF_C) * n2)
    h2v = 6.0 * COEF_C * inv * inv
    h22 = inv * (2.0 * COEF_B + inv * (6.0 * COEF_C) * n2)
    mix = h3v * m3 + h2v * m2
    return (
        h33 * m3 + h32 * m2 - h3v * vm,
        h32 * m3 + h22 * m2 - h2v * vm,
        -mix * vp - h22 * mp,
        -mix * vr - h22 * mr,
        -mix * vc - h22 * mc,
    )


def push_back(q, fields, back_ref, z_ref):
    g3, g2, gp, gr, gc = fields
    stacked = jnp.concatenate([g3, AREA * g2, -VEC * gp, -VEC * gr, -VEC * gc], axis=0)
    high, low = split(stacked)
    z_ref[q + RADIUS] = dot(back_ref[...], jnp.concatenate([high, low], axis=0))


def columns_back(planes, z_ref, cols_ref, d_ref):
    def step(q, carry):
        start = pl.multiple_of(q * ROWS, ROWS)
        for k in range(KINDS):
            total = None
            for place, (kind, off) in enumerate(USED):
                if kind == k:
                    term = z_ref[q + off, place * ROWS : (place + 1) * ROWS, :]
                    total = term if total is None else total + term
            d_ref[pl.ds(start, ROWS), k * WIDE : (k + 1) * WIDE] = total
        return carry

    lax.fori_loop(0, planes, step, 0, unroll=2)
    out = None
    for k in range(KINDS):
        high, low = split(d_ref[:, k * WIDE : (k + 1) * WIDE])
        mat = cols_ref[k * WIDE : (k + 1) * WIDE, :]
        term = dot(high, mat) + dot(low, mat)
        out = term if out is None else out + term
    return out.reshape(planes, ROWS, LANES)


def clear_edges(planes, z_ref):
    zeros = jnp.zeros((RADIUS, N_BACK, WIDE), jnp.float32)
    z_ref[0:RADIUS] = zeros
    z_ref[RADIUS + planes :] = zeros


def first_kernel(
    planes, x_ref, pot_ref, lab_ref, cols_ref, front_ref, back_ref, colsb_ref,
    weight_ref, dens_ref, c_ref, y_ref, z_ref, d_ref,
):
    columns_forward(planes, x_ref, cols_ref, c_ref)
    rows_forward(planes, c_ref, front_ref, y_ref)
    clear_edges(planes, z_ref)

    def step(q, carry):
        dens = densities_at(q, y_ref)
        for i in range(5):
            dens_ref[q, i * MID : (i + 1) * MID, :] = dens[i]
        push_back(q, derivs_of(*dens), back_ref, z_ref)
        return carry

    lax.fori_loop(0, planes, step, 0, unroll=2)
    total = columns_back(planes, z_ref, colsb_ref, d_ref)
    mask = lab_ref[...].astype(jnp.float32)
    weight_ref[...] = mask * jnp.exp(-total - pot_ref[...])


def second_kernel(
    planes, cells, x_ref, dens_ref, rho_ref, sum_ref, rung_ref, table_ref, cols_ref, front_ref, back_ref, colsb_ref,
    out_ref, c_ref, y_ref, z_ref, d_ref,
):
    columns_forward(planes, x_ref, cols_ref, c_ref)
    rows_forward(planes, c_ref, front_ref, y_ref)
    clear_edges(planes, z_ref)

    def step(q, carry):
        images = densities_at(q, y_ref)
        dens = [dens_ref[q, i * MID : (i + 1) * MID, :] for i in range(5)]
        push_back(q, hess_of(dens, images), back_ref, z_ref)
        return carry

    lax.fori_loop(0, planes, step, 0, unroll=2)
    total = columns_back(planes, z_ref, colsb_ref, d_ref)
    weight = x_ref[:, ROWS : 2 * ROWS, 0:LANES]
    rho = rho_ref[:, ROWS : 2 * ROWS, 0:LANES]
    amount = jnp.sum(sum_ref[...], axis=(0, 1), keepdims=True) * (1.0 / cells)
    amount = jnp.broadcast_to(amount, (ROWS, LANES))
    coefficient = jnp.log(amount / pick(rung_ref[0], table_ref)) / amount
    out_ref[...] = coefficient[None] * (rho * total - weight)


def scratch(planes):
    return [
        pltpu.VMEM((planes * TALL, KINDS * WIDE), jnp.float32),
        pltpu.VMEM((planes + 2 * RADIUS, GROUPS * MID, WIDE), jnp.float32),
        pltpu.VMEM((planes + 2 * RADIUS, N_BACK, WIDE), jnp.float32),
        pltpu.VMEM((planes * ROWS, KINDS * WIDE), jnp.float32),
    ]


PARAMS = pltpu.CompilerParams(vmem_limit_bytes=58 * 1024 * 1024)
VM = pl.BlockSpec(memory_space=pltpu.VMEM)
SM = pl.BlockSpec(memory_space=pltpu.SMEM)


MESH = pl.DeviceIdType.MESH


def pick(index, table_ref):
    total = jnp.float32(0.0)
    for i in range(table_ref.shape[0]):
        total = total + jnp.where(index == i, table_ref[i], jnp.float32(0.0))
    return total


def swap_tiles(x_ref, send_sem, recv_sem):
    count = lax.axis_size("ty")
    ty, tx = lax.axis_index("ty"), lax.axis_index("tx")
    own = x_ref.at[:, ROWS : 2 * ROWS, 0:LANES]

    def copy(i, src, rows, lane, device):
        dst = x_ref.at[:, rows : rows + ROWS, lane : lane + LANES]
        return pltpu.make_async_remote_copy(
            src_ref=src, dst_ref=dst, send_sem=send_sem.at[i], recv_sem=recv_sem.at[i],
            device_id=device, device_id_type=MESH,
        )

    beside = {"tx": 1 - tx}
    down = copy(0, own, 0, 0, {"ty": lax.rem(ty + 1, count)})
    up = copy(1, own, 2 * ROWS, 0, {"ty": lax.rem(ty + count - 1, count)})
    side = copy(2, own, ROWS, LANES, beside)
    down.start()
    up.start()
    side.start()
    head = copy(3, x_ref.at[:, 0:ROWS, 0:LANES], 0, LANES, beside)
    tail = copy(4, x_ref.at[:, 2 * ROWS : 3 * ROWS, 0:LANES], 2 * ROWS, LANES, beside)
    down.wait_recv()
    head.start()
    up.wait_recv()
    tail.start()
    down.wait_send()
    up.wait_send()
    side.wait()
    head.wait()
    tail.wait()


def greet(devices):
    barrier = pltpu.get_barrier_semaphore()
    for device in devices:
        pl.semaphore_signal(barrier, inc=1, device_id=device, device_id_type=MESH)
    pl.semaphore_wait(barrier, len(devices))


def start_kernel(pot_ref, lab_ref, rung_ref, table_ref, x_ref, send_sem, recv_sem):
    count = lax.axis_size("ty")
    ty, tx = lax.axis_index("ty"), lax.axis_index("tx")
    chem_pot = pick(rung_ref[0], table_ref)
    mask = lab_ref[...].astype(jnp.float32)
    x_ref[:, ROWS : 2 * ROWS, 0:LANES] = mask * jnp.exp(chem_pot - pot_ref[...])
    greet([
        {"ty": lax.rem(ty + 1, count)}, {"ty": lax.rem(ty + count - 1, count)}, {"tx": 1 - tx},
    ])
    swap_tiles(x_ref, send_sem, recv_sem)


def weight_kernel(
    weight_ref, x_ref, sum_ref, slots, send_sem, recv_sem, part_send, part_recv,
):
    cores = lax.axis_size("tx")
    group = lax.axis_size("ty") * cores
    me = lax.axis_index("ty") * cores + lax.axis_index("tx")
    others = []
    for j in range(1, group):
        target = lax.rem(me + j, group)
        others.append({"ty": target // cores, "tx": lax.rem(target, cores)})
    weight = weight_ref[...]
    x_ref[:, ROWS : 2 * ROWS, 0:LANES] = weight
    slots[0] = jnp.sum(weight, axis=0)
    greet(others)
    copies = []
    for j in range(1, group):
        copies.append(pltpu.make_async_remote_copy(
            src_ref=slots.at[0], dst_ref=slots.at[j],
            send_sem=part_send.at[j], recv_sem=part_recv.at[j],
            device_id=others[j - 1], device_id_type=MESH,
        ))
        copies[-1].start()
    swap_tiles(x_ref, send_sem, recv_sem)
    for copy in copies:
        copy.wait()
    total = slots[0]
    for j in range(1, group):
        total = total + slots[j]
    sum_ref[...] = total


def rung_kernel(grad_ref, out_ref, slots, send_sem, recv_sem):
    count = lax.axis_size("rung")
    me = lax.axis_index("rung")
    others = [{"rung": lax.rem(me + j, count)} for j in range(1, count)]
    greet(others)
    copies = []
    for j in range(1, count):
        copies.append(pltpu.make_async_remote_copy(
            src_ref=grad_ref, dst_ref=slots.at[j - 1],
            send_sem=send_sem.at[j - 1], recv_sem=recv_sem.at[j - 1],
            device_id=others[j - 1], device_id_type=MESH,
        ))
        copies[-1].start()
    for copy in copies:
        copy.wait()
    total = grad_ref[...]
    for j in range(1, count):
        total = total + slots[j - 1]
    out_ref[...] = total


def talks(place):
    return pltpu.CompilerParams(
        collective_id=place, has_side_effects=True, vmem_limit_bytes=24 * 1024 * 1024
    )


def dma(count):
    return pltpu.SemaphoreType.DMA((count,))


def body(potential, labels, rung_mu, mu_table, target_table):
    planes = potential.shape[0]
    group = lax.axis_size("ty") * lax.axis_size("tx")
    rungs = lax.axis_size("rung")
    tile = jax.ShapeDtypeStruct(potential.shape, jnp.float32)
    wide = jax.ShapeDtypeStruct((planes, TALL, WIDE), jnp.float32)
    mats = [jnp.asarray(m) for m in (COLS_FWD, FRONT, BACK, COLS_BACK)]
    rho_wide = pl.pallas_call(
        start_kernel,
        out_shape=wide,
        in_specs=[VM, VM, SM, SM],
        out_specs=VM,
        scratch_shapes=[dma(5), dma(5)],
        compiler_params=talks(0),
    )(potential, labels, rung_mu, mu_table)
    weight, dens = pl.pallas_call(
        functools.partial(first_kernel, planes),
        out_shape=(tile, jax.ShapeDtypeStruct((planes, 5 * MID, WIDE), jnp.float32)),
        in_specs=[VM] * 7,
        out_specs=(VM, VM),
        scratch_shapes=scratch(planes),
        compiler_params=PARAMS,
    )(rho_wide, potential, labels, *mats)
    weight_wide, amounts = pl.pallas_call(
        weight_kernel,
        out_shape=(wide, jax.ShapeDtypeStruct((ROWS, LANES), jnp.float32)),
        in_specs=[VM],
        out_specs=(VM, VM),
        scratch_shapes=[
            pltpu.VMEM((group, ROWS, LANES), jnp.float32),
            dma(5), dma(5), dma(group), dma(group),
        ],
        compiler_params=talks(1),
    )(weight)
    grad = pl.pallas_call(
        functools.partial(second_kernel, planes, potential.size * group),
        out_shape=tile,
        in_specs=[VM] * 4 + [SM] * 2 + [VM] * 4,
        out_specs=VM,
        scratch_shapes=scratch(planes),
        compiler_params=PARAMS,
    )(weight_wide, dens, rho_wide, amounts, rung_mu, target_table, *mats)
    return pl.pallas_call(
        rung_kernel,
        out_shape=tile,
        in_specs=[VM],
        out_specs=VM,
        scratch_shapes=[
            pltpu.VMEM((rungs - 1,) + potential.shape, jnp.float32),
            dma(rungs - 1), dma(rungs - 1),
        ],
        compiler_params=talks(2),
    )(grad)


def solution(mesh):
    return jax.shard_map(
        body,
        mesh=mesh,
        in_specs=(P("parts", "ty", "tx"), P("parts", "ty", "tx"), P(("parts", "rung")), P(), P()),
        out_specs=P("parts", "ty", "tx"),
        check_vma=False,
    )
```

```python
import functools
import math

import numpy as np
import ml_dtypes

import jax
import jax.numpy as jnp
from jax import lax
from jax.experimental import pallas as pl
from jax.experimental.pallas import tpu as pltpu
from jax.sharding import PartitionSpec as P

RADIUS = 4
ROWS = 8
TALL = 24
MID = 16
LANES = 128
WIDE = 256
KINDS = 2 * RADIUS + 1
DEPTH = 224
BOX_IN = (RADIUS + 1) * TALL
BOX_OUT = 3 * (RADIUS + 1) * MID
COEF_A = 1.0 / (4.0 * math.pi * RADIUS * RADIUS)
COEF_B = 1.0 / (4.0 * math.pi * RADIUS)
COEF_C = 1.0 / (24.0 * math.pi)


def reach_of(allowed, factor, radius):
    height = -1
    for candidate in range(radius + 1):
        if factor * candidate * candidate <= allowed:
            height = candidate
    return height


def span_count(height):
    return 2 * height + 1 if height >= 0 else 0


def reaches(plane_off, row_off):
    square = plane_off * plane_off + row_off * row_off
    ball = reach_of(RADIUS * RADIUS - square, 1, RADIUS)
    inner = reach_of((2 * RADIUS - 1) ** 2 - 4 * square, 4, RADIUS)
    outer = reach_of((2 * RADIUS + 1) ** 2 - 4 * square, 4, RADIUS)
    return ball, inner, outer


OFFS = range(-RADIUS, RADIUS + 1)
SHELL = sum(
    span_count(reaches(p, s)[2]) - span_count(reaches(p, s)[1]) for p in OFFS for s in OFFS
)
AREA = 4.0 * math.pi * RADIUS * RADIUS / SHELL
VEC = AREA / RADIUS


def shell_terms(p, s):
    _, inner, outer = reaches(p, s)
    terms = []
    if outer >= 0:
        terms.append((outer, 1))
    if inner >= 0:
        terms.append((inner, -1))
    return terms


def column_matrix():
    mat = np.zeros((KINDS, WIDE, WIDE), np.float32)
    for out in range(WIDE):
        for h in OFFS:
            src = (out + h) % WIDE
            for k in range(abs(h), RADIUS + 1):
                mat[k, src, out] = 1
                if k > 0:
                    mat[RADIUS + k, src, out] = h
    return mat


def spread_rows():
    mat = np.zeros((4, RADIUS + 1, MID, DEPTH), np.float32)
    for p in range(RADIUS + 1):
        for s in OFFS:
            ball = reaches(p, s)[0]
            for r in range(MID):
                src = r + RADIUS + s
                if ball >= 0:
                    mat[0, p, r, ball * TALL + src] += 1
                for k, sign in shell_terms(p, s):
                    mat[1, p, r, k * TALL + src] += sign
                    mat[2, p, r, k * TALL + src] += s * sign
                    if k > 0:
                        mat[3, p, r, (RADIUS + k) * TALL + src] += sign
    flat = mat.reshape(4 * (RADIUS + 1) * MID, DEPTH)
    box = flat[:BOX_OUT, :BOX_IN]
    moment = flat[BOX_OUT:, BOX_IN : KINDS * TALL]
    return np.concatenate([box, box], axis=1), np.concatenate([moment, moment], axis=1)


def collect_rows():
    full = np.zeros((KINDS, KINDS, ROWS, 5 * MID), np.float32)
    for p in OFFS:
        for s in OFFS:
            ball = reaches(p, s)[0]
            for r in range(ROWS):
                src = r + RADIUS + s
                if ball >= 0:
                    full[ball, p + RADIUS, r, src] += 1
                for k, sign in shell_terms(p, s):
                    full[k, p + RADIUS, r, MID + src] += sign
                    full[k, p + RADIUS, r, 2 * MID + src] += p * sign
                    full[k, p + RADIUS, r, 3 * MID + src] += s * sign
                    if k > 0:
                        full[RADIUS + k, p + RADIUS, r, 4 * MID + src] += sign
    used = [(k, p) for k in range(KINDS) for p in range(KINDS) if np.any(full[k, p])]
    flat = np.concatenate([full[k, p] for k, p in used], axis=0)
    return used, np.concatenate([flat, flat], axis=1)


COLS = column_matrix()
USED, BACK = collect_rows()
GROUPS = 4 * (RADIUS + 1)
BF = ml_dtypes.bfloat16
COLS_FWD = np.concatenate([COLS[k] for k in range(1, KINDS)], axis=1).astype(BF)
COLS_BACK = np.concatenate([COLS[k][:, :LANES] for k in range(KINDS)], axis=0).astype(BF)
FRONT_BOX, FRONT_MOM = [m.astype(BF) for m in spread_rows()]
BACK = BACK.astype(BF)
N_BACK = len(USED) * ROWS


def split(x):
    high = x.astype(jnp.bfloat16)
    low = (x - high.astype(jnp.float32)).astype(jnp.bfloat16)
    return high, low


def dot(a, b):
    return jnp.dot(a, b, preferred_element_type=jnp.float32)


def columns_forward(planes, x_ref, cols_ref, c_ref):
    x = x_ref[...].reshape(planes * TALL, WIDE)
    c_ref[:, 0:WIDE] = x
    high, low = split(x)
    for k in range(1, KINDS):
        mat = cols_ref[:, (k - 1) * WIDE : k * WIDE]
        c_ref[:, k * WIDE : (k + 1) * WIDE] = dot(high, mat) + dot(low, mat)


def stack_parts(x):
    high = x.astype(jnp.bfloat16).astype(jnp.float32)
    return jnp.concatenate([high, x - high], axis=0).astype(jnp.bfloat16)


def rows_forward(planes, c_ref, box_ref, mom_ref, y_ref):
    zeros = jnp.zeros((RADIUS, GROUPS * MID, WIDE), jnp.float32)
    y_ref[0:RADIUS] = zeros
    y_ref[RADIUS + planes :] = zeros

    def step(q, carry):
        start = pl.multiple_of(q * TALL, TALL)
        parts = [c_ref[pl.ds(start, TALL), k * WIDE : (k + 1) * WIDE] for k in range(KINDS)]
        boxes = jnp.concatenate(parts[: RADIUS + 1], axis=0)
        moments = jnp.concatenate(parts[RADIUS + 1 :], axis=0)
        y_ref[q + RADIUS, 0:BOX_OUT, :] = dot(box_ref[...], stack_parts(boxes))
        y_ref[q + RADIUS, BOX_OUT:, :] = dot(mom_ref[...], stack_parts(moments))
        return carry

    lax.fori_loop(0, planes, step, 0, unroll=4)


def densities_at(q, y_ref):
    def get(group, p, off):
        row = (group * (RADIUS + 1) + p) * MID
        return y_ref[q + RADIUS + off, row : row + MID, :]

    volume, surface, rows, cols = [get(g, 0, 0) for g in range(4)]
    plane = jnp.zeros_like(volume)
    for p in range(1, RADIUS + 1):
        volume = volume + (get(0, p, p) + get(0, p, -p))
        after, before = get(1, p, p), get(1, p, -p)
        surface = surface + (after + before)
        plane = plane + p * (after - before)
        rows = rows + (get(2, p, p) + get(2, p, -p))
        cols = cols + (get(3, p, p) + get(3, p, -p))
    return volume, AREA * surface, VEC * plane, VEC * rows, VEC * cols


def derivs_of(n3, n2, vp, vr, vc):
    free = 1.0 - n3
    inv = 1.0 / free
    sq = vp * vp + vr * vr + vc * vc
    u = n2 * n2 - sq
    w = n2 * (u - 2.0 * sq)
    d3 = inv * (COEF_A * n2 + inv * (COEF_B * u + inv * (2.0 * COEF_C) * w))
    d2 = -COEF_A * jnp.log(free) + inv * (2.0 * COEF_B * n2 + inv * (3.0 * COEF_C) * u)
    dv = -inv * (2.0 * COEF_B + inv * (6.0 * COEF_C) * n2)
    return d3, d2, dv * vp, dv * vr, dv * vc


def hess_of(dens, images):
    n3, n2, vp, vr, vc = dens
    m3, m2, mp, mr, mc = images
    inv = 1.0 / (1.0 - n3)
    sq = vp * vp + vr * vr + vc * vc
    u = n2 * n2 - sq
    w = n2 * (u - 2.0 * sq)
    vm = vp * mp + vr * mr + vc * mc
    h33 = inv * inv * (COEF_A * n2 + inv * (2.0 * COEF_B * u + inv * (6.0 * COEF_C) * w))
    h32 = inv * (COEF_A + inv * (2.0 * COEF_B * n2 + inv * (6.0 * COEF_C) * u))
    h3v = inv * inv * (2.0 * COEF_B + inv * (12.0 * COEF_C) * n2)
    h2v = 6.0 * COEF_C * inv * inv
    h22 = inv * (2.0 * COEF_B + inv * (6.0 * COEF_C) * n2)
    mix = h3v * m3 + h2v * m2
    return (
        h33 * m3 + h32 * m2 - h3v * vm,
        h32 * m3 + h22 * m2 - h2v * vm,
        -mix * vp - h22 * mp,
        -mix * vr - h22 * mr,
        -mix * vc - h22 * mc,
    )


def push_back(q, fields, back_ref, z_ref):
    g3, g2, gp, gr, gc = fields
    stacked = jnp.concatenate([g3, AREA * g2, -VEC * gp, -VEC * gr, -VEC * gc], axis=0)
    high, low = split(stacked)
    z_ref[q + RADIUS] = dot(back_ref[...], jnp.concatenate([high, low], axis=0))


def columns_back(planes, z_ref, cols_ref, d_ref):
    def step(q, carry):
        start = pl.multiple_of(q * ROWS, ROWS)
        for k in range(KINDS):
            total = None
            for place, (kind, off) in enumerate(USED):
                if kind == k:
                    term = z_ref[q + off, place * ROWS : (place + 1) * ROWS, :]
                    total = term if total is None else total + term
            d_ref[pl.ds(start, ROWS), k * WIDE : (k + 1) * WIDE] = total
        return carry

    lax.fori_loop(0, planes, step, 0, unroll=2)
    out = None
    for k in range(KINDS):
        high, low = split(d_ref[:, k * WIDE : (k + 1) * WIDE])
        mat = cols_ref[k * WIDE : (k + 1) * WIDE, :]
        term = dot(high, mat) + dot(low, mat)
        out = term if out is None else out + term
    return out.reshape(planes, ROWS, LANES)


def clear_edges(planes, z_ref):
    zeros = jnp.zeros((RADIUS, N_BACK, WIDE), jnp.float32)
    z_ref[0:RADIUS] = zeros
    z_ref[RADIUS + planes :] = zeros


def first_kernel(
    planes, x_ref, pot_ref, lab_ref, cols_ref, box_ref, mom_ref, back_ref, colsb_ref,
    weight_ref, dens_ref, c_ref, y_ref, z_ref, d_ref,
):
    columns_forward(planes, x_ref, cols_ref, c_ref)
    rows_forward(planes, c_ref, box_ref, mom_ref, y_ref)
    clear_edges(planes, z_ref)

    def step(q, carry):
        dens = densities_at(q, y_ref)
        for i in range(5):
            dens_ref[q, i * MID : (i + 1) * MID, :] = dens[i]
        push_back(q, derivs_of(*dens), back_ref, z_ref)
        return carry

    lax.fori_loop(0, planes, step, 0, unroll=2)
    total = columns_back(planes, z_ref, colsb_ref, d_ref)
    mask = lab_ref[...].astype(jnp.float32)
    weight_ref[...] = mask * jnp.exp(-total - pot_ref[...])


def second_kernel(
    planes, cells, x_ref, dens_ref, rho_ref, sum_ref, rung_ref, table_ref, cols_ref, box_ref, mom_ref, back_ref, colsb_ref,
    out_ref, c_ref, y_ref, z_ref, d_ref,
):
    columns_forward(planes, x_ref, cols_ref, c_ref)
    rows_forward(planes, c_ref, box_ref, mom_ref, y_ref)
    clear_edges(planes, z_ref)

    def step(q, carry):
        images = densities_at(q, y_ref)
        dens = [dens_ref[q, i * MID : (i + 1) * MID, :] for i in range(5)]
        push_back(q, hess_of(dens, images), back_ref, z_ref)
        return carry

    lax.fori_loop(0, planes, step, 0, unroll=2)
    total = columns_back(planes, z_ref, colsb_ref, d_ref)
    weight = x_ref[:, ROWS : 2 * ROWS, 0:LANES]
    rho = rho_ref[:, ROWS : 2 * ROWS, 0:LANES]
    amount = jnp.sum(sum_ref[...], axis=(0, 1), keepdims=True) * (1.0 / cells)
    amount = jnp.broadcast_to(amount, (ROWS, LANES))
    coefficient = jnp.log(amount / pick(rung_ref[0], table_ref)) / amount
    out_ref[...] = coefficient[None] * (rho * total - weight)


def scratch(planes):
    return [
        pltpu.VMEM((planes * TALL, KINDS * WIDE), jnp.float32),
        pltpu.VMEM((planes + 2 * RADIUS, GROUPS * MID, WIDE), jnp.float32),
        pltpu.VMEM((planes + 2 * RADIUS, N_BACK, WIDE), jnp.float32),
        pltpu.VMEM((planes * ROWS, KINDS * WIDE), jnp.float32),
    ]


PARAMS = pltpu.CompilerParams(vmem_limit_bytes=47 * 1024 * 1024)
COST = pl.CostEstimate(flops=5_000_000_000, bytes_accessed=30_000_000, transcendentals=0)
VM = pl.BlockSpec(memory_space=pltpu.VMEM)
SM = pl.BlockSpec(memory_space=pltpu.SMEM)


MESH = pl.DeviceIdType.MESH


def pick(index, table_ref):
    total = jnp.float32(0.0)
    for i in range(table_ref.shape[0]):
        total = total + jnp.where(index == i, table_ref[i], jnp.float32(0.0))
    return total


def swap_tiles(x_ref, send_sem, recv_sem):
    count = lax.axis_size("ty")
    ty, tx = lax.axis_index("ty"), lax.axis_index("tx")
    own = x_ref.at[:, ROWS : 2 * ROWS, 0:LANES]

    def copy(i, src, rows, lane, device):
        dst = x_ref.at[:, rows : rows + ROWS, lane : lane + LANES]
        return pltpu.make_async_remote_copy(
            src_ref=src, dst_ref=dst, send_sem=send_sem.at[i], recv_sem=recv_sem.at[i],
            device_id=device, device_id_type=MESH,
        )

    beside = {"tx": 1 - tx}
    down = copy(0, own, 0, 0, {"ty": lax.rem(ty + 1, count)})
    up = copy(1, own, 2 * ROWS, 0, {"ty": lax.rem(ty + count - 1, count)})
    side = copy(2, own, ROWS, LANES, beside)
    down.start()
    up.start()
    side.start()
    head = copy(3, x_ref.at[:, 0:ROWS, 0:LANES], 0, LANES, beside)
    tail = copy(4, x_ref.at[:, 2 * ROWS : 3 * ROWS, 0:LANES], 2 * ROWS, LANES, beside)
    down.wait_recv()
    head.start()
    up.wait_recv()
    tail.start()
    down.wait_send()
    up.wait_send()
    side.wait()
    head.wait()
    tail.wait()


def greet(devices):
    barrier = pltpu.get_barrier_semaphore()
    for device in devices:
        pl.semaphore_signal(barrier, inc=1, device_id=device, device_id_type=MESH)
    pl.semaphore_wait(barrier, len(devices))


def start_kernel(pot_ref, lab_ref, rung_ref, table_ref, x_ref, send_sem, recv_sem):
    count = lax.axis_size("ty")
    ty, tx = lax.axis_index("ty"), lax.axis_index("tx")
    chem_pot = pick(rung_ref[0], table_ref)
    mask = lab_ref[...].astype(jnp.float32)
    x_ref[:, ROWS : 2 * ROWS, 0:LANES] = mask * jnp.exp(chem_pot - pot_ref[...])
    greet([
        {"ty": lax.rem(ty + 1, count)}, {"ty": lax.rem(ty + count - 1, count)}, {"tx": 1 - tx},
    ])
    swap_tiles(x_ref, send_sem, recv_sem)


def weight_kernel(
    weight_ref, x_ref, sum_ref, slots, send_sem, recv_sem, part_send, part_recv,
):
    cores = lax.axis_size("tx")
    group = lax.axis_size("ty") * cores
    me = lax.axis_index("ty") * cores + lax.axis_index("tx")
    others = []
    for j in range(1, group):
        target = lax.rem(me + j, group)
        others.append({"ty": target // cores, "tx": lax.rem(target, cores)})
    weight = weight_ref[...]
    x_ref[:, ROWS : 2 * ROWS, 0:LANES] = weight
    slots[0] = jnp.sum(weight, axis=0)
    greet(others)
    copies = []
    for j in range(1, group):
        copies.append(pltpu.make_async_remote_copy(
            src_ref=slots.at[0], dst_ref=slots.at[j],
            send_sem=part_send.at[j], recv_sem=part_recv.at[j],
            device_id=others[j - 1], device_id_type=MESH,
        ))
        copies[-1].start()
    swap_tiles(x_ref, send_sem, recv_sem)
    for copy in copies:
        copy.wait()
    total = slots[0]
    for j in range(1, group):
        total = total + slots[j]
    sum_ref[...] = total


def rung_kernel(grad_ref, out_ref, slots, send_sem, recv_sem):
    count = lax.axis_size("rung")
    me = lax.axis_index("rung")
    others = [{"rung": lax.rem(me + j, count)} for j in range(1, count)]
    greet(others)
    copies = []
    for j in range(1, count):
        copies.append(pltpu.make_async_remote_copy(
            src_ref=grad_ref, dst_ref=slots.at[j - 1],
            send_sem=send_sem.at[j - 1], recv_sem=recv_sem.at[j - 1],
            device_id=others[j - 1], device_id_type=MESH,
        ))
        copies[-1].start()
    for copy in copies:
        copy.wait()
    total = grad_ref[...]
    for j in range(1, count):
        total = total + slots[j - 1]
    out_ref[...] = total


def talks(place):
    return pltpu.CompilerParams(
        collective_id=place, has_side_effects=True, vmem_limit_bytes=8 * 1024 * 1024
    )


def dma(count):
    return pltpu.SemaphoreType.DMA((count,))


def body(potential, labels, rung_mu, mu_table, target_table):
    planes = potential.shape[0]
    group = lax.axis_size("ty") * lax.axis_size("tx")
    rungs = lax.axis_size("rung")
    tile = jax.ShapeDtypeStruct(potential.shape, jnp.float32)
    wide = jax.ShapeDtypeStruct((planes, TALL, WIDE), jnp.float32)
    mats = [jnp.asarray(m) for m in (COLS_FWD, FRONT_BOX, FRONT_MOM, BACK, COLS_BACK)]
    rho_wide = pl.pallas_call(
        start_kernel,
        out_shape=wide,
        in_specs=[VM, VM, SM, SM],
        out_specs=VM,
        scratch_shapes=[dma(5), dma(5)],
        compiler_params=talks(0),
        cost_estimate=COST,
    )(potential, labels, rung_mu, mu_table)
    weight, dens = pl.pallas_call(
        functools.partial(first_kernel, planes),
        out_shape=(tile, jax.ShapeDtypeStruct((planes, 5 * MID, WIDE), jnp.float32)),
        in_specs=[VM] * 8,
        out_specs=(VM, VM),
        scratch_shapes=scratch(planes),
        compiler_params=PARAMS,
        cost_estimate=COST,
    )(rho_wide, potential, labels, *mats)
    weight_wide, amounts = pl.pallas_call(
        weight_kernel,
        out_shape=(wide, jax.ShapeDtypeStruct((ROWS, LANES), jnp.float32)),
        in_specs=[VM],
        out_specs=(VM, VM),
        scratch_shapes=[
            pltpu.VMEM((group, ROWS, LANES), jnp.float32),
            dma(5), dma(5), dma(group), dma(group),
        ],
        compiler_params=talks(1),
        cost_estimate=COST,
    )(weight)
    grad = pl.pallas_call(
        functools.partial(second_kernel, planes, potential.size * group),
        out_shape=tile,
        in_specs=[VM] * 4 + [SM] * 2 + [VM] * 5,
        out_specs=VM,
        scratch_shapes=scratch(planes),
        compiler_params=PARAMS,
        cost_estimate=COST,
    )(weight_wide, dens, rho_wide, amounts, rung_mu, target_table, *mats)
    return pl.pallas_call(
        rung_kernel,
        out_shape=tile,
        in_specs=[VM],
        out_specs=VM,
        scratch_shapes=[
            pltpu.VMEM((rungs - 1,) + potential.shape, jnp.float32),
            dma(rungs - 1), dma(rungs - 1),
        ],
        compiler_params=talks(2),
        cost_estimate=COST,
    )(grad)


def solution(mesh):
    return jax.shard_map(
        body,
        mesh=mesh,
        in_specs=(P("parts", "ty", "tx"), P("parts", "ty", "tx"), P(("parts", "rung")), P(), P()),
        out_specs=P("parts", "ty", "tx"),
        check_vma=False,
    )
```

```python
import functools
import math

import numpy as np
import ml_dtypes

import jax
import jax.numpy as jnp
from jax import lax
from jax.experimental import pallas as pl
from jax.experimental.pallas import tpu as pltpu
from jax.sharding import PartitionSpec as P

RADIUS = 4
ROWS = 8
TALL = 24
MID = 16
LANES = 128
WIDE = 256
KINDS = 2 * RADIUS + 1
DEPTH = 224
BOX_IN = (RADIUS + 1) * TALL
BOX_OUT = 3 * (RADIUS + 1) * MID
COEF_A = 1.0 / (4.0 * math.pi * RADIUS * RADIUS)
COEF_B = 1.0 / (4.0 * math.pi * RADIUS)
COEF_C = 1.0 / (24.0 * math.pi)


def reach_of(allowed, factor, radius):
    height = -1
    for candidate in range(radius + 1):
        if factor * candidate * candidate <= allowed:
            height = candidate
    return height


def span_count(height):
    return 2 * height + 1 if height >= 0 else 0


def reaches(plane_off, row_off):
    square = plane_off * plane_off + row_off * row_off
    ball = reach_of(RADIUS * RADIUS - square, 1, RADIUS)
    inner = reach_of((2 * RADIUS - 1) ** 2 - 4 * square, 4, RADIUS)
    outer = reach_of((2 * RADIUS + 1) ** 2 - 4 * square, 4, RADIUS)
    return ball, inner, outer


OFFS = range(-RADIUS, RADIUS + 1)
SHELL = sum(
    span_count(reaches(p, s)[2]) - span_count(reaches(p, s)[1]) for p in OFFS for s in OFFS
)
AREA = 4.0 * math.pi * RADIUS * RADIUS / SHELL
VEC = AREA / RADIUS


def shell_terms(p, s):
    _, inner, outer = reaches(p, s)
    terms = []
    if outer >= 0:
        terms.append((outer, 1))
    if inner >= 0:
        terms.append((inner, -1))
    return terms


def column_matrix():
    mat = np.zeros((KINDS, WIDE, WIDE), np.float32)
    for out in range(WIDE):
        for h in OFFS:
            src = (out + h) % WIDE
            for k in range(abs(h), RADIUS + 1):
                mat[k, src, out] = 1
                if k > 0:
                    mat[RADIUS + k, src, out] = h
    return mat


def spread_rows():
    mat = np.zeros((4, RADIUS + 1, MID, DEPTH), np.float32)
    for p in range(RADIUS + 1):
        for s in OFFS:
            ball = reaches(p, s)[0]
            for r in range(MID):
                src = r + RADIUS + s
                if ball >= 0:
                    mat[0, p, r, ball * TALL + src] += 1
                for k, sign in shell_terms(p, s):
                    mat[1, p, r, k * TALL + src] += sign
                    mat[2, p, r, k * TALL + src] += s * sign
                    if k > 0:
                        mat[3, p, r, (RADIUS + k) * TALL + src] += sign
    flat = mat.reshape(4 * (RADIUS + 1) * MID, DEPTH)
    box = flat[:BOX_OUT, :BOX_IN]
    moment = flat[BOX_OUT:, BOX_IN : KINDS * TALL]
    return np.concatenate([box, box], axis=1), np.concatenate([moment, moment], axis=1)


def collect_rows():
    full = np.zeros((KINDS, KINDS, ROWS, 5 * MID), np.float32)
    for p in OFFS:
        for s in OFFS:
            ball = reaches(p, s)[0]
            for r in range(ROWS):
                src = r + RADIUS + s
                if ball >= 0:
                    full[ball, p + RADIUS, r, src] += 1
                for k, sign in shell_terms(p, s):
                    full[k, p + RADIUS, r, MID + src] += sign
                    full[k, p + RADIUS, r, 2 * MID + src] += p * sign
                    full[k, p + RADIUS, r, 3 * MID + src] += s * sign
                    if k > 0:
                        full[RADIUS + k, p + RADIUS, r, 4 * MID + src] += sign
    used = [(k, p) for k in range(KINDS) for p in range(KINDS) if np.any(full[k, p])]
    flat = np.concatenate([full[k, p] for k, p in used], axis=0)
    return used, np.concatenate([flat, flat], axis=1)


COLS = column_matrix()
USED, BACK = collect_rows()
GROUPS = 4 * (RADIUS + 1)
BF = ml_dtypes.bfloat16
COLS_FWD = np.concatenate([COLS[k] for k in range(1, KINDS)], axis=1).astype(BF)
COLS_BACK = np.concatenate([COLS[k][:, :LANES] for k in range(KINDS)], axis=0).astype(BF)
FRONT_BOX, FRONT_MOM = [m.astype(BF) for m in spread_rows()]
BACK = BACK.astype(BF)
N_BACK = len(USED) * ROWS


def split(x):
    high = x.astype(jnp.bfloat16)
    low = (x - high.astype(jnp.float32)).astype(jnp.bfloat16)
    return high, low


def dot(a, b):
    return jnp.dot(a, b, preferred_element_type=jnp.float32)


def columns_forward(planes, x_ref, cols_ref, c_ref):
    strips = [jnp.concatenate([x_ref[b], x_ref[b + 1]], axis=2) for b in (0, 2, 4)]
    x = jnp.concatenate(strips, axis=1).reshape(planes * TALL, WIDE)
    c_ref[:, 0:WIDE] = x
    high, low = split(x)
    for k in range(1, KINDS):
        mat = cols_ref[:, (k - 1) * WIDE : k * WIDE]
        c_ref[:, k * WIDE : (k + 1) * WIDE] = dot(high, mat) + dot(low, mat)


def stack_parts(x):
    high = x.astype(jnp.bfloat16).astype(jnp.float32)
    return jnp.concatenate([high, x - high], axis=0).astype(jnp.bfloat16)


def rows_forward(planes, c_ref, box_ref, mom_ref, y_ref):
    zeros = jnp.zeros((RADIUS, GROUPS * MID, WIDE), jnp.float32)
    y_ref[0:RADIUS] = zeros
    y_ref[RADIUS + planes :] = zeros

    def step(q, carry):
        start = pl.multiple_of(q * TALL, TALL)
        parts = [c_ref[pl.ds(start, TALL), k * WIDE : (k + 1) * WIDE] for k in range(KINDS)]
        boxes = jnp.concatenate(parts[: RADIUS + 1], axis=0)
        moments = jnp.concatenate(parts[RADIUS + 1 :], axis=0)
        y_ref[q + RADIUS, 0:BOX_OUT, :] = dot(box_ref[...], stack_parts(boxes))
        y_ref[q + RADIUS, BOX_OUT:, :] = dot(mom_ref[...], stack_parts(moments))
        return carry

    lax.fori_loop(0, planes, step, 0, unroll=4)


def densities_at(q, y_ref):
    def get(group, p, off):
        row = (group * (RADIUS + 1) + p) * MID
        return y_ref[q + RADIUS + off, row : row + MID, :]

    volume, surface, rows, cols = [get(g, 0, 0) for g in range(4)]
    plane = jnp.zeros_like(volume)
    for p in range(1, RADIUS + 1):
        volume = volume + (get(0, p, p) + get(0, p, -p))
        after, before = get(1, p, p), get(1, p, -p)
        surface = surface + (after + before)
        plane = plane + p * (after - before)
        rows = rows + (get(2, p, p) + get(2, p, -p))
        cols = cols + (get(3, p, p) + get(3, p, -p))
    return volume, AREA * surface, VEC * plane, VEC * rows, VEC * cols


def derivs_of(n3, n2, vp, vr, vc):
    free = 1.0 - n3
    inv = 1.0 / free
    sq = vp * vp + vr * vr + vc * vc
    u = n2 * n2 - sq
    w = n2 * (u - 2.0 * sq)
    d3 = inv * (COEF_A * n2 + inv * (COEF_B * u + inv * (2.0 * COEF_C) * w))
    d2 = -COEF_A * jnp.log(free) + inv * (2.0 * COEF_B * n2 + inv * (3.0 * COEF_C) * u)
    dv = -inv * (2.0 * COEF_B + inv * (6.0 * COEF_C) * n2)
    return d3, d2, dv * vp, dv * vr, dv * vc


def hess_of(dens, images):
    n3, n2, vp, vr, vc = dens
    m3, m2, mp, mr, mc = images
    inv = 1.0 / (1.0 - n3)
    sq = vp * vp + vr * vr + vc * vc
    u = n2 * n2 - sq
    w = n2 * (u - 2.0 * sq)
    vm = vp * mp + vr * mr + vc * mc
    h33 = inv * inv * (COEF_A * n2 + inv * (2.0 * COEF_B * u + inv * (6.0 * COEF_C) * w))
    h32 = inv * (COEF_A + inv * (2.0 * COEF_B * n2 + inv * (6.0 * COEF_C) * u))
    h3v = inv * inv * (2.0 * COEF_B + inv * (12.0 * COEF_C) * n2)
    h2v = 6.0 * COEF_C * inv * inv
    h22 = inv * (2.0 * COEF_B + inv * (6.0 * COEF_C) * n2)
    mix = h3v * m3 + h2v * m2
    return (
        h33 * m3 + h32 * m2 - h3v * vm,
        h32 * m3 + h22 * m2 - h2v * vm,
        -mix * vp - h22 * mp,
        -mix * vr - h22 * mr,
        -mix * vc - h22 * mc,
    )


def push_back(q, fields, back_ref, z_ref):
    g3, g2, gp, gr, gc = fields
    stacked = jnp.concatenate([g3, AREA * g2, -VEC * gp, -VEC * gr, -VEC * gc], axis=0)
    high, low = split(stacked)
    z_ref[q + RADIUS] = dot(back_ref[...], jnp.concatenate([high, low], axis=0))


def columns_back(planes, z_ref, cols_ref, d_ref):
    def step(q, carry):
        start = pl.multiple_of(q * ROWS, ROWS)
        for k in range(KINDS):
            total = None
            for place, (kind, off) in enumerate(USED):
                if kind == k:
                    term = z_ref[q + off, place * ROWS : (place + 1) * ROWS, :]
                    total = term if total is None else total + term
            d_ref[pl.ds(start, ROWS), k * WIDE : (k + 1) * WIDE] = total
        return carry

    lax.fori_loop(0, planes, step, 0, unroll=2)
    out = None
    for k in range(KINDS):
        high, low = split(d_ref[:, k * WIDE : (k + 1) * WIDE])
        mat = cols_ref[k * WIDE : (k + 1) * WIDE, :]
        term = dot(high, mat) + dot(low, mat)
        out = term if out is None else out + term
    return out.reshape(planes, ROWS, LANES)


def clear_edges(planes, z_ref):
    zeros = jnp.zeros((RADIUS, N_BACK, WIDE), jnp.float32)
    z_ref[0:RADIUS] = zeros
    z_ref[RADIUS + planes :] = zeros


def first_kernel(
    planes, x_ref, pot_ref, lab_ref, cols_ref, box_ref, mom_ref, back_ref, colsb_ref,
    weight_ref, dens_ref, c_ref, y_ref, z_ref, d_ref,
):
    columns_forward(planes, x_ref, cols_ref, c_ref)
    rows_forward(planes, c_ref, box_ref, mom_ref, y_ref)
    clear_edges(planes, z_ref)

    def step(q, carry):
        dens = densities_at(q, y_ref)
        for i in range(5):
            dens_ref[q, i * MID : (i + 1) * MID, :] = dens[i]
        push_back(q, derivs_of(*dens), back_ref, z_ref)
        return carry

    lax.fori_loop(0, planes, step, 0, unroll=2)
    total = columns_back(planes, z_ref, colsb_ref, d_ref)
    mask = lab_ref[...].astype(jnp.float32)
    weight_ref[...] = mask * jnp.exp(-total - pot_ref[...])


def second_kernel(
    planes, cells, x_ref, dens_ref, rho_ref, sum_ref, rung_ref, table_ref, cols_ref, box_ref, mom_ref, back_ref, colsb_ref,
    out_ref, c_ref, y_ref, z_ref, d_ref,
):
    columns_forward(planes, x_ref, cols_ref, c_ref)
    rows_forward(planes, c_ref, box_ref, mom_ref, y_ref)
    clear_edges(planes, z_ref)

    def step(q, carry):
        images = densities_at(q, y_ref)
        dens = [dens_ref[q, i * MID : (i + 1) * MID, :] for i in range(5)]
        push_back(q, hess_of(dens, images), back_ref, z_ref)
        return carry

    lax.fori_loop(0, planes, step, 0, unroll=2)
    total = columns_back(planes, z_ref, colsb_ref, d_ref)
    weight = x_ref[2]
    rho = rho_ref[2]
    amount = jnp.sum(sum_ref[...], axis=(0, 1), keepdims=True) * (1.0 / cells)
    amount = jnp.broadcast_to(amount, (ROWS, LANES))
    coefficient = jnp.log(amount / pick(rung_ref[0], table_ref)) / amount
    out_ref[...] = coefficient[None] * (rho * total - weight)


def scratch(planes):
    return [
        pltpu.VMEM((planes * TALL, KINDS * WIDE), jnp.float32),
        pltpu.VMEM((planes + 2 * RADIUS, GROUPS * MID, WIDE), jnp.float32),
        pltpu.VMEM((planes + 2 * RADIUS, N_BACK, WIDE), jnp.float32),
        pltpu.VMEM((planes * ROWS, KINDS * WIDE), jnp.float32),
    ]


PARAMS = pltpu.CompilerParams(vmem_limit_bytes=47 * 1024 * 1024)
COST = pl.CostEstimate(flops=5_000_000_000, bytes_accessed=30_000_000, transcendentals=0)
VM = pl.BlockSpec(memory_space=pltpu.VMEM)
SM = pl.BlockSpec(memory_space=pltpu.SMEM)


MESH = pl.DeviceIdType.MESH
CHUNKS = 2


def pick(index, table_ref):
    total = jnp.float32(0.0)
    for i in range(table_ref.shape[0]):
        total = total + jnp.where(index == i, table_ref[i], jnp.float32(0.0))
    return total


def swap_tiles(x_ref, send_sem, recv_sem):
    count = lax.axis_size("ty")
    ty, tx = lax.axis_index("ty"), lax.axis_index("tx")
    size = x_ref.shape[1] // CHUNKS

    def copy(i, chunk, src, dst, device):
        place = pl.ds(chunk * size, size)
        return pltpu.make_async_remote_copy(
            src_ref=x_ref.at[src, place], dst_ref=x_ref.at[dst, place],
            send_sem=send_sem.at[i * CHUNKS + chunk], recv_sem=recv_sem.at[i * CHUNKS + chunk],
            device_id=device, device_id_type=MESH,
        )

    chunks = range(CHUNKS)
    beside = {"tx": 1 - tx}
    down = [copy(0, c, 2, 0, {"ty": lax.rem(ty + 1, count)}) for c in chunks]
    up = [copy(1, c, 2, 4, {"ty": lax.rem(ty + count - 1, count)}) for c in chunks]
    side = [copy(2, c, 2, 3, beside) for c in chunks]
    head = [copy(3, c, 0, 1, beside) for c in chunks]
    tail = [copy(4, c, 4, 5, beside) for c in chunks]
    for c in chunks:
        down[c].start()
        up[c].start()
    for c in chunks:
        side[c].start()
    for c in chunks:
        down[c].wait_recv()
        head[c].start()
        up[c].wait_recv()
        tail[c].start()
    for c in chunks:
        down[c].wait_send()
        up[c].wait_send()
        side[c].wait()
        head[c].wait()
        tail[c].wait()


def greet(devices):
    barrier = pltpu.get_barrier_semaphore()
    for device in devices:
        pl.semaphore_signal(barrier, inc=1, device_id=device, device_id_type=MESH)
    pl.semaphore_wait(barrier, len(devices))


def start_kernel(
    pot_ref, lab_ref, rung_ref, table_ref, x_ref, send_sem, recv_sem,
):
    count = lax.axis_size("ty")
    ty, tx = lax.axis_index("ty"), lax.axis_index("tx")
    greet([
        {"ty": lax.rem(ty + 1, count)}, {"ty": lax.rem(ty + count - 1, count)}, {"tx": 1 - tx},
    ])
    chem_pot = pick(rung_ref[0], table_ref)
    mask = lab_ref[...].astype(jnp.float32)
    x_ref[2] = mask * jnp.exp(chem_pot - pot_ref[...])
    swap_tiles(x_ref, send_sem, recv_sem)


def weight_kernel(
    weight_ref, x_ref, sum_ref, slots, send_sem, recv_sem, part_send, part_recv,
):
    cores = lax.axis_size("tx")
    group = lax.axis_size("ty") * cores
    me = lax.axis_index("ty") * cores + lax.axis_index("tx")
    others = []
    for j in range(1, group):
        target = lax.rem(me + j, group)
        others.append({"ty": target // cores, "tx": lax.rem(target, cores)})
    weight = weight_ref[...]
    x_ref[2] = weight
    slots[0] = jnp.sum(weight, axis=0)
    greet(others)
    copies = []
    for j in range(1, group):
        copies.append(pltpu.make_async_remote_copy(
            src_ref=slots.at[0], dst_ref=slots.at[j],
            send_sem=part_send.at[j], recv_sem=part_recv.at[j],
            device_id=others[j - 1], device_id_type=MESH,
        ))
        copies[-1].start()
    swap_tiles(x_ref, send_sem, recv_sem)
    for copy in copies:
        copy.wait()
    total = slots[0]
    for j in range(1, group):
        total = total + slots[j]
    sum_ref[...] = total


def rung_kernel(grad_ref, out_ref, slots, send_sem, recv_sem):
    count = lax.axis_size("rung")
    me = lax.axis_index("rung")
    others = [{"rung": lax.rem(me + j, count)} for j in range(1, count)]
    greet(others)
    copies = []
    for j in range(1, count):
        copies.append(pltpu.make_async_remote_copy(
            src_ref=grad_ref, dst_ref=slots.at[j - 1],
            send_sem=send_sem.at[j - 1], recv_sem=recv_sem.at[j - 1],
            device_id=others[j - 1], device_id_type=MESH,
        ))
        copies[-1].start()
    for copy in copies:
        copy.wait()
    total = grad_ref[...]
    for j in range(1, count):
        total = total + slots[j - 1]
    out_ref[...] = total


def talks(place):
    return pltpu.CompilerParams(
        collective_id=place, has_side_effects=True, vmem_limit_bytes=8 * 1024 * 1024
    )


def dma(count):
    return pltpu.SemaphoreType.DMA((count,))


def body(potential, labels, rung_mu, mu_table, target_table):
    planes = potential.shape[0]
    group = lax.axis_size("ty") * lax.axis_size("tx")
    rungs = lax.axis_size("rung")
    tile = jax.ShapeDtypeStruct(potential.shape, jnp.float32)
    wide = jax.ShapeDtypeStruct((6,) + potential.shape, jnp.float32)
    mats = [jnp.asarray(m) for m in (COLS_FWD, FRONT_BOX, FRONT_MOM, BACK, COLS_BACK)]
    rho_wide = pl.pallas_call(
        start_kernel,
        out_shape=wide,
        in_specs=[VM, VM, SM, SM],
        out_specs=VM,
        scratch_shapes=[
            dma(5 * CHUNKS), dma(5 * CHUNKS),
        ],
        compiler_params=talks(0),
        cost_estimate=COST,
    )(potential, labels, rung_mu, mu_table)
    weight, dens = pl.pallas_call(
        functools.partial(first_kernel, planes),
        out_shape=(tile, jax.ShapeDtypeStruct((planes, 5 * MID, WIDE), jnp.float32)),
        in_specs=[VM] * 8,
        out_specs=(VM, VM),
        scratch_shapes=scratch(planes),
        compiler_params=PARAMS,
        cost_estimate=COST,
    )(rho_wide, potential, labels, *mats)
    weight_wide, amounts = pl.pallas_call(
        weight_kernel,
        out_shape=(wide, jax.ShapeDtypeStruct((ROWS, LANES), jnp.float32)),
        in_specs=[VM],
        out_specs=(VM, VM),
        scratch_shapes=[
            pltpu.VMEM((group, ROWS, LANES), jnp.float32),
            dma(5 * CHUNKS), dma(5 * CHUNKS), dma(group), dma(group),
        ],
        compiler_params=talks(1),
        cost_estimate=COST,
    )(weight)
    grad = pl.pallas_call(
        functools.partial(second_kernel, planes, potential.size * group),
        out_shape=tile,
        in_specs=[VM] * 4 + [SM] * 2 + [VM] * 5,
        out_specs=VM,
        scratch_shapes=scratch(planes),
        compiler_params=PARAMS,
        cost_estimate=COST,
    )(weight_wide, dens, rho_wide, amounts, rung_mu, target_table, *mats)
    return pl.pallas_call(
        rung_kernel,
        out_shape=tile,
        in_specs=[VM],
        out_specs=VM,
        scratch_shapes=[
            pltpu.VMEM((rungs - 1,) + potential.shape, jnp.float32),
            dma(rungs - 1), dma(rungs - 1),
        ],
        compiler_params=talks(2),
        cost_estimate=COST,
    )(grad)


def solution(mesh):
    return jax.shard_map(
        body,
        mesh=mesh,
        in_specs=(P("parts", "ty", "tx"), P("parts", "ty", "tx"), P(("parts", "rung")), P(), P()),
        out_specs=P("parts", "ty", "tx"),
        check_vma=False,
    )
```

```python
import functools
import math

import numpy as np
import ml_dtypes

import jax
import jax.numpy as jnp
from jax import lax
from jax.experimental import pallas as pl
from jax.experimental.pallas import tpu as pltpu
from jax.sharding import PartitionSpec as P

RADIUS = 4
ROWS = 8
TALL = 24
MID = 16
LANES = 128
WIDE = 256
KINDS = 2 * RADIUS + 1
DEPTH = 224
BOX_IN = (RADIUS + 1) * TALL
BOX_OUT = 3 * (RADIUS + 1) * MID
COEF_A = 1.0 / (4.0 * math.pi * RADIUS * RADIUS)
COEF_B = 1.0 / (4.0 * math.pi * RADIUS)
COEF_C = 1.0 / (24.0 * math.pi)


def reach_of(allowed, factor, radius):
    height = -1
    for candidate in range(radius + 1):
        if factor * candidate * candidate <= allowed:
            height = candidate
    return height


def span_count(height):
    return 2 * height + 1 if height >= 0 else 0


def reaches(plane_off, row_off):
    square = plane_off * plane_off + row_off * row_off
    ball = reach_of(RADIUS * RADIUS - square, 1, RADIUS)
    inner = reach_of((2 * RADIUS - 1) ** 2 - 4 * square, 4, RADIUS)
    outer = reach_of((2 * RADIUS + 1) ** 2 - 4 * square, 4, RADIUS)
    return ball, inner, outer


OFFS = range(-RADIUS, RADIUS + 1)
SHELL = sum(
    span_count(reaches(p, s)[2]) - span_count(reaches(p, s)[1]) for p in OFFS for s in OFFS
)
AREA = 4.0 * math.pi * RADIUS * RADIUS / SHELL
VEC = AREA / RADIUS


def shell_terms(p, s):
    _, inner, outer = reaches(p, s)
    terms = []
    if outer >= 0:
        terms.append((outer, 1))
    if inner >= 0:
        terms.append((inner, -1))
    return terms


def column_matrix():
    mat = np.zeros((KINDS, WIDE, WIDE), np.float32)
    for out in range(WIDE):
        for h in OFFS:
            src = (out + h) % WIDE
            for k in range(abs(h), RADIUS + 1):
                mat[k, src, out] = 1
                if k > 0:
                    mat[RADIUS + k, src, out] = h
    return mat


def spread_rows():
    mat = np.zeros((4, RADIUS + 1, MID, DEPTH), np.float32)
    for p in range(RADIUS + 1):
        for s in OFFS:
            ball = reaches(p, s)[0]
            for r in range(MID):
                src = r + RADIUS + s
                if ball >= 0:
                    mat[0, p, r, ball * TALL + src] += 1
                for k, sign in shell_terms(p, s):
                    mat[1, p, r, k * TALL + src] += sign
                    mat[2, p, r, k * TALL + src] += s * sign
                    if k > 0:
                        mat[3, p, r, (RADIUS + k) * TALL + src] += sign
    flat = mat.reshape(4 * (RADIUS + 1) * MID, DEPTH)
    box = flat[:BOX_OUT, :BOX_IN]
    moment = flat[BOX_OUT:, BOX_IN : KINDS * TALL]
    return np.concatenate([box, box], axis=1), np.concatenate([moment, moment], axis=1)


def collect_rows():
    full = np.zeros((KINDS, KINDS, ROWS, 5 * MID), np.float32)
    for p in OFFS:
        for s in OFFS:
            ball = reaches(p, s)[0]
            for r in range(ROWS):
                src = r + RADIUS + s
                if ball >= 0:
                    full[ball, p + RADIUS, r, src] += 1
                for k, sign in shell_terms(p, s):
                    full[k, p + RADIUS, r, MID + src] += sign
                    full[k, p + RADIUS, r, 2 * MID + src] += p * sign
                    full[k, p + RADIUS, r, 3 * MID + src] += s * sign
                    if k > 0:
                        full[RADIUS + k, p + RADIUS, r, 4 * MID + src] += sign
    used = [(k, p) for k in range(KINDS) for p in range(KINDS) if np.any(full[k, p])]
    flat = np.concatenate([full[k, p] for k, p in used], axis=0)
    return used, np.concatenate([flat, flat], axis=1)


COLS = column_matrix()
USED, BACK = collect_rows()
GROUPS = 4 * (RADIUS + 1)
BF = ml_dtypes.bfloat16
COLS_FWD = np.concatenate([COLS[k] for k in range(1, KINDS)], axis=1).astype(BF)
COLS_BACK = np.concatenate([COLS[k][:, :LANES] for k in range(KINDS)], axis=0).astype(BF)
FRONT_BOX, FRONT_MOM = [m.astype(BF) for m in spread_rows()]
BACK = BACK.astype(BF)
N_BACK = len(USED) * ROWS


def split(x):
    high = x.astype(jnp.bfloat16)
    low = (x - high.astype(jnp.float32)).astype(jnp.bfloat16)
    return high, low


def dot(a, b):
    return jnp.dot(a, b, preferred_element_type=jnp.float32)


def columns_forward(planes, x_ref, cols_ref, c_ref):
    x = x_ref[...].reshape(planes * TALL, WIDE)
    c_ref[:, 0:WIDE] = x
    high, low = split(x)
    for k in range(1, KINDS):
        mat = cols_ref[:, (k - 1) * WIDE : k * WIDE]
        c_ref[:, k * WIDE : (k + 1) * WIDE] = dot(high, mat) + dot(low, mat)


def stack_parts(x):
    high = x.astype(jnp.bfloat16).astype(jnp.float32)
    return jnp.concatenate([high, x - high], axis=0).astype(jnp.bfloat16)


def rows_forward(planes, c_ref, box_ref, mom_ref, y_ref):
    zeros = jnp.zeros((RADIUS, GROUPS * MID, WIDE), jnp.float32)
    y_ref[0:RADIUS] = zeros
    y_ref[RADIUS + planes :] = zeros

    def step(q, carry):
        start = pl.multiple_of(q * TALL, TALL)
        parts = [c_ref[pl.ds(start, TALL), k * WIDE : (k + 1) * WIDE] for k in range(KINDS)]
        boxes = jnp.concatenate(parts[: RADIUS + 1], axis=0)
        moments = jnp.concatenate(parts[RADIUS + 1 :], axis=0)
        y_ref[q + RADIUS, 0:BOX_OUT, :] = dot(box_ref[...], stack_parts(boxes))
        y_ref[q + RADIUS, BOX_OUT:, :] = dot(mom_ref[...], stack_parts(moments))
        return carry

    lax.fori_loop(0, planes, step, 0, unroll=4)


def densities_at(q, y_ref):
    def get(group, p, off):
        row = (group * (RADIUS + 1) + p) * MID
        return y_ref[q + RADIUS + off, row : row + MID, :]

    volume, surface, rows, cols = [get(g, 0, 0) for g in range(4)]
    plane = jnp.zeros_like(volume)
    for p in range(1, RADIUS + 1):
        volume = volume + (get(0, p, p) + get(0, p, -p))
        after, before = get(1, p, p), get(1, p, -p)
        surface = surface + (after + before)
        plane = plane + p * (after - before)
        rows = rows + (get(2, p, p) + get(2, p, -p))
        cols = cols + (get(3, p, p) + get(3, p, -p))
    return volume, AREA * surface, VEC * plane, VEC * rows, VEC * cols


def derivs_of(n3, n2, vp, vr, vc):
    free = 1.0 - n3
    inv = 1.0 / free
    sq = vp * vp + vr * vr + vc * vc
    u = n2 * n2 - sq
    w = n2 * (u - 2.0 * sq)
    d3 = inv * (COEF_A * n2 + inv * (COEF_B * u + inv * (2.0 * COEF_C) * w))
    d2 = -COEF_A * jnp.log(free) + inv * (2.0 * COEF_B * n2 + inv * (3.0 * COEF_C) * u)
    dv = -inv * (2.0 * COEF_B + inv * (6.0 * COEF_C) * n2)
    return d3, d2, dv * vp, dv * vr, dv * vc


def hess_of(dens, images):
    n3, n2, vp, vr, vc = dens
    m3, m2, mp, mr, mc = images
    inv = 1.0 / (1.0 - n3)
    sq = vp * vp + vr * vr + vc * vc
    u = n2 * n2 - sq
    w = n2 * (u - 2.0 * sq)
    vm = vp * mp + vr * mr + vc * mc
    h33 = inv * inv * (COEF_A * n2 + inv * (2.0 * COEF_B * u + inv * (6.0 * COEF_C) * w))
    h32 = inv * (COEF_A + inv * (2.0 * COEF_B * n2 + inv * (6.0 * COEF_C) * u))
    h3v = inv * inv * (2.0 * COEF_B + inv * (12.0 * COEF_C) * n2)
    h2v = 6.0 * COEF_C * inv * inv
    h22 = inv * (2.0 * COEF_B + inv * (6.0 * COEF_C) * n2)
    mix = h3v * m3 + h2v * m2
    return (
        h33 * m3 + h32 * m2 - h3v * vm,
        h32 * m3 + h22 * m2 - h2v * vm,
        -mix * vp - h22 * mp,
        -mix * vr - h22 * mr,
        -mix * vc - h22 * mc,
    )


def push_back(q, fields, back_ref, z_ref):
    g3, g2, gp, gr, gc = fields
    stacked = jnp.concatenate([g3, AREA * g2, -VEC * gp, -VEC * gr, -VEC * gc], axis=0)
    high, low = split(stacked)
    z_ref[q + RADIUS] = dot(back_ref[...], jnp.concatenate([high, low], axis=0))


def columns_back(planes, z_ref, cols_ref, d_ref):
    def step(q, carry):
        start = pl.multiple_of(q * ROWS, ROWS)
        for k in range(KINDS):
            total = None
            for place, (kind, off) in enumerate(USED):
                if kind == k:
                    term = z_ref[q + off, place * ROWS : (place + 1) * ROWS, :]
                    total = term if total is None else total + term
            d_ref[pl.ds(start, ROWS), k * WIDE : (k + 1) * WIDE] = total
        return carry

    lax.fori_loop(0, planes, step, 0, unroll=4)
    out = None
    for k in range(KINDS):
        high, low = split(d_ref[:, k * WIDE : (k + 1) * WIDE])
        mat = cols_ref[k * WIDE : (k + 1) * WIDE, :]
        term = dot(high, mat) + dot(low, mat)
        out = term if out is None else out + term
    return out.reshape(planes, ROWS, LANES)


def clear_edges(planes, z_ref):
    zeros = jnp.zeros((RADIUS, N_BACK, WIDE), jnp.float32)
    z_ref[0:RADIUS] = zeros
    z_ref[RADIUS + planes :] = zeros


def first_kernel(
    planes, x_ref, pot_ref, lab_ref, cols_ref, box_ref, mom_ref, back_ref, colsb_ref,
    weight_ref, dens_ref, c_ref, y_ref, z_ref, d_ref,
):
    columns_forward(planes, x_ref, cols_ref, c_ref)
    rows_forward(planes, c_ref, box_ref, mom_ref, y_ref)
    clear_edges(planes, z_ref)

    def step(q, carry):
        dens = densities_at(q, y_ref)
        for i in range(5):
            dens_ref[q, i * MID : (i + 1) * MID, :] = dens[i]
        push_back(q, derivs_of(*dens), back_ref, z_ref)
        return carry

    lax.fori_loop(0, planes, step, 0, unroll=4)
    total = columns_back(planes, z_ref, colsb_ref, d_ref)
    mask = lab_ref[...].astype(jnp.float32)
    weight_ref[...] = mask * jnp.exp(-total - pot_ref[...])


def second_kernel(
    planes, cells, x_ref, dens_ref, rho_ref, sum_ref, rung_ref, table_ref, cols_ref, box_ref, mom_ref, back_ref, colsb_ref,
    out_ref, c_ref, y_ref, z_ref, d_ref,
):
    columns_forward(planes, x_ref, cols_ref, c_ref)
    rows_forward(planes, c_ref, box_ref, mom_ref, y_ref)
    clear_edges(planes, z_ref)

    def step(q, carry):
        images = densities_at(q, y_ref)
        dens = [dens_ref[q, i * MID : (i + 1) * MID, :] for i in range(5)]
        push_back(q, hess_of(dens, images), back_ref, z_ref)
        return carry

    lax.fori_loop(0, planes, step, 0, unroll=4)
    total = columns_back(planes, z_ref, colsb_ref, d_ref)
    weight = x_ref[:, ROWS : 2 * ROWS, 0:LANES]
    rho = rho_ref[:, ROWS : 2 * ROWS, 0:LANES]
    amount = jnp.sum(sum_ref[...], axis=(0, 1), keepdims=True) * (1.0 / cells)
    amount = jnp.broadcast_to(amount, (ROWS, LANES))
    coefficient = jnp.log(amount / pick(rung_ref[0], table_ref)) / amount
    out_ref[...] = coefficient[None] * (rho * total - weight)


def scratch(planes):
    return [
        pltpu.VMEM((planes * TALL, KINDS * WIDE), jnp.float32),
        pltpu.VMEM((planes + 2 * RADIUS, GROUPS * MID, WIDE), jnp.float32),
        pltpu.VMEM((planes + 2 * RADIUS, N_BACK, WIDE), jnp.float32),
        pltpu.VMEM((planes * ROWS, KINDS * WIDE), jnp.float32),
    ]


PARAMS = pltpu.CompilerParams(vmem_limit_bytes=47 * 1024 * 1024)
COST = pl.CostEstimate(flops=5_000_000_000, bytes_accessed=30_000_000, transcendentals=0)
VM = pl.BlockSpec(memory_space=pltpu.VMEM)
SM = pl.BlockSpec(memory_space=pltpu.SMEM)


MESH = pl.DeviceIdType.MESH


def pick(index, table_ref):
    total = jnp.float32(0.0)
    for i in range(table_ref.shape[0]):
        total = total + jnp.where(index == i, table_ref[i], jnp.float32(0.0))
    return total


def swap_tiles(x_ref, send_sem, recv_sem):
    count = lax.axis_size("ty")
    ty, tx = lax.axis_index("ty"), lax.axis_index("tx")
    own = x_ref.at[:, ROWS : 2 * ROWS, 0:LANES]

    def copy(i, src, rows, lane, device):
        dst = x_ref.at[:, rows : rows + ROWS, lane : lane + LANES]
        return pltpu.make_async_remote_copy(
            src_ref=src, dst_ref=dst, send_sem=send_sem.at[i], recv_sem=recv_sem.at[i],
            device_id=device, device_id_type=MESH,
        )

    beside = {"tx": 1 - tx}
    down = copy(0, own, 0, 0, {"ty": lax.rem(ty + 1, count)})
    up = copy(1, own, 2 * ROWS, 0, {"ty": lax.rem(ty + count - 1, count)})
    side = copy(2, own, ROWS, LANES, beside)
    down.start()
    up.start()
    side.start()
    head = copy(3, x_ref.at[:, 0:ROWS, 0:LANES], 0, LANES, beside)
    tail = copy(4, x_ref.at[:, 2 * ROWS : 3 * ROWS, 0:LANES], 2 * ROWS, LANES, beside)
    down.wait_recv()
    head.start()
    up.wait_recv()
    tail.start()
    down.wait_send()
    up.wait_send()
    side.wait()
    head.wait()
    tail.wait()


def greet(devices):
    barrier = pltpu.get_barrier_semaphore()
    for device in devices:
        pl.semaphore_signal(barrier, inc=1, device_id=device, device_id_type=MESH)
    pl.semaphore_wait(barrier, len(devices))


def start_kernel(pot_ref, lab_ref, rung_ref, table_ref, x_ref, send_sem, recv_sem):
    count = lax.axis_size("ty")
    ty, tx = lax.axis_index("ty"), lax.axis_index("tx")
    chem_pot = pick(rung_ref[0], table_ref)
    mask = lab_ref[...].astype(jnp.float32)
    x_ref[:, ROWS : 2 * ROWS, 0:LANES] = mask * jnp.exp(chem_pot - pot_ref[...])
    greet([
        {"ty": lax.rem(ty + 1, count)}, {"ty": lax.rem(ty + count - 1, count)}, {"tx": 1 - tx},
    ])
    swap_tiles(x_ref, send_sem, recv_sem)


def weight_kernel(
    weight_ref, x_ref, sum_ref, slots, send_sem, recv_sem, part_send, part_recv,
):
    cores = lax.axis_size("tx")
    group = lax.axis_size("ty") * cores
    me = lax.axis_index("ty") * cores + lax.axis_index("tx")
    others = []
    for j in range(1, group):
        target = lax.rem(me + j, group)
        others.append({"ty": target // cores, "tx": lax.rem(target, cores)})
    weight = weight_ref[...]
    x_ref[:, ROWS : 2 * ROWS, 0:LANES] = weight
    slots[0] = jnp.sum(weight, axis=0)
    greet(others)
    copies = []
    for j in range(1, group):
        copies.append(pltpu.make_async_remote_copy(
            src_ref=slots.at[0], dst_ref=slots.at[j],
            send_sem=part_send.at[j], recv_sem=part_recv.at[j],
            device_id=others[j - 1], device_id_type=MESH,
        ))
        copies[-1].start()
    swap_tiles(x_ref, send_sem, recv_sem)
    for copy in copies:
        copy.wait()
    total = slots[0]
    for j in range(1, group):
        total = total + slots[j]
    sum_ref[...] = total


def rung_kernel(grad_ref, out_ref, slots, send_sem, recv_sem):
    count = lax.axis_size("rung")
    me = lax.axis_index("rung")
    others = [{"rung": lax.rem(me + j, count)} for j in range(1, count)]
    greet(others)
    copies = []
    for j in range(1, count):
        copies.append(pltpu.make_async_remote_copy(
            src_ref=grad_ref, dst_ref=slots.at[j - 1],
            send_sem=send_sem.at[j - 1], recv_sem=recv_sem.at[j - 1],
            device_id=others[j - 1], device_id_type=MESH,
        ))
        copies[-1].start()
    for copy in copies:
        copy.wait()
    total = grad_ref[...]
    for j in range(1, count):
        total = total + slots[j - 1]
    out_ref[...] = total


def talks(place):
    return pltpu.CompilerParams(
        collective_id=place, has_side_effects=True, vmem_limit_bytes=8 * 1024 * 1024
    )


def dma(count):
    return pltpu.SemaphoreType.DMA((count,))


def body(potential, labels, rung_mu, mu_table, target_table):
    planes = potential.shape[0]
    group = lax.axis_size("ty") * lax.axis_size("tx")
    rungs = lax.axis_size("rung")
    tile = jax.ShapeDtypeStruct(potential.shape, jnp.float32)
    wide = jax.ShapeDtypeStruct((planes, TALL, WIDE), jnp.float32)
    mats = [jnp.asarray(m) for m in (COLS_FWD, FRONT_BOX, FRONT_MOM, BACK, COLS_BACK)]
    rho_wide = pl.pallas_call(
        start_kernel,
        out_shape=wide,
        in_specs=[VM, VM, SM, SM],
        out_specs=VM,
        scratch_shapes=[dma(5), dma(5)],
        compiler_params=talks(0),
        cost_estimate=COST,
    )(potential, labels, rung_mu, mu_table)
    weight, dens = pl.pallas_call(
        functools.partial(first_kernel, planes),
        out_shape=(tile, jax.ShapeDtypeStruct((planes, 5 * MID, WIDE), jnp.float32)),
        in_specs=[VM] * 8,
        out_specs=(VM, VM),
        scratch_shapes=scratch(planes),
        compiler_params=PARAMS,
        cost_estimate=COST,
    )(rho_wide, potential, labels, *mats)
    weight_wide, amounts = pl.pallas_call(
        weight_kernel,
        out_shape=(wide, jax.ShapeDtypeStruct((ROWS, LANES), jnp.float32)),
        in_specs=[VM],
        out_specs=(VM, VM),
        scratch_shapes=[
            pltpu.VMEM((group, ROWS, LANES), jnp.float32),
            dma(5), dma(5), dma(group), dma(group),
        ],
        compiler_params=talks(1),
        cost_estimate=COST,
    )(weight)
    grad = pl.pallas_call(
        functools.partial(second_kernel, planes, potential.size * group),
        out_shape=tile,
        in_specs=[VM] * 4 + [SM] * 2 + [VM] * 5,
        out_specs=VM,
        scratch_shapes=scratch(planes),
        compiler_params=PARAMS,
        cost_estimate=COST,
    )(weight_wide, dens, rho_wide, amounts, rung_mu, target_table, *mats)
    return pl.pallas_call(
        rung_kernel,
        out_shape=tile,
        in_specs=[VM],
        out_specs=VM,
        scratch_shapes=[
            pltpu.VMEM((rungs - 1,) + potential.shape, jnp.float32),
            dma(rungs - 1), dma(rungs - 1),
        ],
        compiler_params=talks(2),
        cost_estimate=COST,
    )(grad)


def solution(mesh):
    return jax.shard_map(
        body,
        mesh=mesh,
        in_specs=(P("parts", "ty", "tx"), P("parts", "ty", "tx"), P(("parts", "rung")), P(), P()),
        out_specs=P("parts", "ty", "tx"),
        check_vma=False,
    )
```
